128 devices in a mesh: ia: 32 (over x_hi, y, z), ja: 4 (over x_lo, core).
Axes of the slice: x: 4 (x_hi: 2, x_lo: 2; x = x_hi * 2 + x_lo), y: 4, z: 4, core: 2. Of those that a mesh axis runs over, the one named last changes fastest.
Arguments:
- field: float32 [2, 75, 128, 4096], P(None, None, 'ja', 'ia'), may hold values from -30 to 30
- diff_i: float32 [2, 75, 128, 4096], P(None, None, 'ja', 'ia'), may hold values from 0.5 to 8
- diff_j: float32 [2, 75, 128, 4096], P(None, None, 'ja', 'ia'), may hold values from 0.5 to 8
- land_sea: int32 [75, 128, 4096], P(None, 'ja', 'ia'), may hold values 0 or 1
- partner: int32 [4096], replicated, may hold values from 0 to 4095, as said below
- vertical: float32 [2, 75, 75], replicated, may hold values from -0.5 to 2
Outputs:
- correlated: float32 [2, 75, 128, 4096], P(None, None, 'ja', 'ia')
The draws below stay inside these ranges and needn't reach their ends.
Inputs may be any that keep to these rules, and one draw needn't show every extreme that they name: partner[i] = (c - i) mod 4096 for one column c that is the same for every i, so partner[partner[i]] = i.
All inputs are finite; a program needn't handle non-finite values. No bound on the sum of `land_sea` on one device may be relied on, other than what follows from the above.
Results may differ from the reference program's by a relative error of at most 0.000082.
Values sent between devices are 32-bit elements; how exact they have to be, the bound alone decides.
No kernel may reach another device: no remote copies, remote signals or barrier semaphores. Data moves between devices by JAX's collectives and lax.ppermute only.
A program may use at most 192 MiB of HBM per device.

```python
import math
import jax
import jax.numpy as jnp
from jax import lax

V = 2
L = 75
ITERS = 4
NI = 4096
NJ = 128


def draw_partner(key, part):
    key = jax.random.fold_in(key, 11)
    centre = jax.random.randint(key, (), 0, NI)
    return ((centre - jnp.arange(NI, dtype=jnp.int32)) % NI).astype(jnp.int32)


def draw_vertical(key, part):
    key = jax.random.fold_in(key, 12)
    level_axis = jnp.arange(L, dtype=jnp.float32)
    spacing = jnp.abs(level_axis[:, None] - level_axis[None, :])
    jitter = jnp.clip(0.1 * jax.random.normal(key, (V, L, L)), -0.5, 0.5)
    matrix = jnp.eye(L, dtype=jnp.float32)[None] + 0.5 * jnp.exp(-spacing / 8.0)[None] + jitter
    return matrix.astype(jnp.float32)


def place_ends(result, own_key, low, high):
    place = [jax.random.randint(jax.random.fold_in(own_key, axis), (), 0, length) for axis, length in enumerate(result.shape)]
    widest = result.shape.index(max(result.shape))
    neighbour = place[:widest] + [(place[widest] + 1) % result.shape[widest]] + place[widest + 1:]
    return result.at[tuple(place)].set(low).at[tuple(neighbour)].set(high)


def shard_levels(rng, extent, cuts, least, high):
    def one(position, parts):
        steps = jax.random.uniform(jax.random.fold_in(jax.random.fold_in(rng, 6), position), (parts,), jnp.float32, least / len(cuts), high / len(cuts))
        return jnp.repeat(jnp.exp(steps), extent[position] // parts).reshape((-1,) + (1,) * (len(extent) - position - 1))

    level = one(*cuts[0])
    for cut in cuts[1:]:
        level = level * one(*cut)
    return level


def bell_draw(own_key, dims, spread, most, pieces=(), kind=jnp.bfloat16):
    values = jax.random.normal(own_key, dims, jnp.float32) * spread
    if len(pieces) > 0:
        values = shard_levels(own_key, dims, pieces, -0.22, 0.18) * values
    return jnp.clip(values, min=-most, max=most).astype(kind)


def setup_inputs(seed: int = 0) -> dict:
    streams_of = jax.random.split(jax.random.key(seed), 7)
    field = bell_draw(streams_of[0], (V, L, NJ, NI), 5.0, 30.0, ((2, 4), (3, 32)), jnp.float32)
    diff_i = jnp.clip(jnp.exp(math.log(8.0) - 2.7725887 * jax.random.uniform(streams_of[1], (V, L, NJ, NI), jnp.float32) ** shard_levels(streams_of[1], (V, L, NJ, NI), ((2, 4), (3, 32)), -0.2, 0.2)), 0.5, 8.0)
    diff_j = jnp.clip(jnp.exp(math.log(8.0) - 2.7725887 * jax.random.uniform(streams_of[2], (V, L, NJ, NI), jnp.float32) ** shard_levels(streams_of[2], (V, L, NJ, NI), ((2, 4), (3, 32)), -0.2, 0.2)), 0.5, 8.0)
    land_sea = place_ends((jax.random.randint(streams_of[3], (L, NJ, NI), 0, 8) < 7).astype(jnp.int32), jax.random.fold_in(streams_of[3], 1), 0, 1)
    partner = draw_partner(jax.random.fold_in(streams_of[6], 71), 0)
    vertical = draw_vertical(jax.random.fold_in(streams_of[6], 71), 0)
    return {"field": field, "diff_i": diff_i, "diff_j": diff_j, "land_sea": land_sea, "partner": partner, "vertical": vertical}


diff_ceiling = 8.0

def chebyshev_steps(count):
    lowest_eig = 1.0
    highest_eig = 1.0 + 8.0 * diff_ceiling
    centre_val = 0.5 * (highest_eig + lowest_eig)
    half_width = 0.5 * (highest_eig - lowest_eig)
    plan = []
    step_size = 1.0 / centre_val
    momentum = 0.0
    plan.append((step_size, momentum))
    for turn_index in range(1, count):
        if turn_index == 1:
            momentum = 0.5 * (half_width * step_size) ** 2
        else:
            momentum = (0.5 * half_width * step_size) ** 2
        step_size = 1.0 / (centre_val - momentum / step_size)
        plan.append((step_size, momentum))
    return plan

def sides_of(values, partner):
    east_side = jnp.roll(values, -1, axis=1)
    west_side = jnp.roll(values, 1, axis=1)
    top_row = jnp.take(values[-1:, :], partner, axis=1)
    north_side = jnp.concatenate([values[1:], top_row], axis=0)
    south_side = jnp.concatenate([jnp.zeros_like(values[:1]), values[:-1]], axis=0)
    return (east_side, west_side, north_side, south_side)

def operate(values, partner, zonal_root, zonal_sides, merid_root, merid_sides):
    east_side, west_side, north_side, south_side = sides_of(values, partner)
    zonal_part = zonal_root * (zonal_sides[0] * (values - east_side) + zonal_sides[1] * (values - west_side))
    merid_part = merid_root * (merid_sides[2] * (values - north_side) + merid_sides[3] * (values - south_side))
    return values + zonal_part + merid_part

def reference(field, diff_i, diff_j, land_sea, partner, vertical):
    wet_cells = land_sea.astype(jnp.float32)
    levels = jnp.arange(V * L, dtype=jnp.int32) % L
    plan = chebyshev_steps(ITERS)

    def diffuse_slice(slice_args):
        source, zonal_diff, merid_diff, level = slice_args
        wet_slice = lax.dynamic_index_in_dim(wet_cells, level, 0, keepdims=False)
        zonal_root = jnp.sqrt(zonal_diff) * wet_slice
        merid_root = jnp.sqrt(merid_diff) * wet_slice
        zonal_sides = sides_of(zonal_root, partner)
        merid_sides = sides_of(merid_root, partner)
        source = source * wet_slice
        iterate = jnp.zeros_like(source)
        residual = source
        direction = jnp.zeros_like(source)
        for turn_index in range(ITERS):
            step_size, momentum = plan[turn_index]
            direction = residual + momentum * direction
            iterate = iterate + step_size * direction
            if turn_index < ITERS - 1:
                image = operate(direction, partner, zonal_root, zonal_sides, merid_root, merid_sides)
                residual = residual - step_size * image
        return iterate
    diffused = lax.map(diffuse_slice, (field.reshape(V * L, NJ, NI), diff_i.reshape(V * L, NJ, NI), diff_j.reshape(V * L, NJ, NI), levels))
    diffused = diffused.reshape(V, L, NJ, NI)
    mixed = jnp.einsum('vlm,vmji->vlji', vertical, diffused, precision=lax.Precision.HIGHEST)
    return mixed * wet_cells[None]
```

```python
import functools
import numpy as np
import jax
import jax.numpy as jnp
from jax import lax
from jax.experimental import pallas as pl
from jax.experimental.pallas import tpu as pltpu
from jax.sharding import PartitionSpec as P

ITERS = 4
diff_ceiling = 8.0
V, L, R, C = 2, 75, 32, 128
TILES = 10
LAST = L - 8
SLOTS = 8 * TILES
CENTRE, HALF = 33.0, 32.0
ROOT_SCALE = 32.0**-0.5


def chebyshev_steps(count):
    lowest_eig = 1.0
    highest_eig = 1.0 + 8.0 * diff_ceiling
    centre_val = 0.5 * (highest_eig + lowest_eig)
    half_width = 0.5 * (highest_eig - lowest_eig)
    plan = []
    step_size = 1.0 / centre_val
    momentum = 0.0
    plan.append((step_size, momentum))
    for turn_index in range(1, count):
        if turn_index == 1:
            momentum = 0.5 * (half_width * step_size) ** 2
        else:
            momentum = (0.5 * half_width * step_size) ** 2
        step_size = 1.0 / (centre_val - momentum / step_size)
        plan.append((step_size, momentum))
    return plan


def polynomial():
    poly = np.polynomial.polynomial
    operator = np.array([CENTRE, HALF])
    iterate = np.zeros(1)
    residual = np.ones(1)
    direction = np.zeros(1)
    for turn_index, (step_size, momentum) in enumerate(chebyshev_steps(ITERS)):
        direction = poly.polyadd(residual, momentum * direction)
        iterate = poly.polyadd(iterate, step_size * direction)
        if turn_index < ITERS - 1:
            residual = poly.polysub(residual, step_size * poly.polymul(operator, direction))
    return [float(c) for c in iterate]


POLY = polynomial()
LEAD = POLY[3]
B2, B1, B0 = POLY[2] / LEAD, POLY[1] / LEAD, POLY[0] / LEAD

GHOST = [(0, 1), (0, 2), (0, 3), (1, 1), (1, 2), (2, 1), (2, 2), (2, 3)]


def lanes():
    return lax.broadcasted_iota(jnp.int32, (8, C), 1)


def tile_start(k):
    return jnp.minimum(8 * k, LAST)


def cell(refs, start, r):
    field, diff_i, diff_j, land = refs
    at = pl.ds(start * R + r, 8, stride=R)
    wet = land[at, :].astype(jnp.float32)
    scaled = wet * ROOT_SCALE
    return (
        field[0, at, :] * wet,
        jnp.sqrt(diff_i[0, at, :]) * scaled,
        jnp.sqrt(diff_j[0, at, :]) * scaled,
    )


def slot_of(lane):
    return ((lane + 3) & 127) >> 3


def pack_kernel(meta, field, diff_i, diff_j, land, send_a, send_b, send_e, send_o):
    i_odd = meta[0] == 1
    j_odd = meta[1] == 1
    refs = (field, diff_i, diff_j, land)
    lane = lanes()
    slot = slot_of(lane)
    low = (lane & 7) < 4

    def tile(k, carry):
        start = tile_start(k)
        rows = pl.ds(pl.multiple_of(8 * k, 8), 8)
        packed = [[jnp.zeros((8, C), jnp.float32) for _ in range(2)] for _ in range(3)]
        kept = {}
        for r in range(R):
            values = cell(refs, start, r)
            if r < 3 or r >= R - 3:
                kept[r] = values
            half, index = divmod(r, 16)
            for a in range(3):
                moved = pltpu.roll(values[a], 8 * index, 1) if index else values[a]
                packed[a][half] = jnp.where(slot == index, moved, packed[a][half])
        for a in range(3):
            first, second = packed[a]
            left = jnp.where(low, first, pltpu.roll(second, 4, 1))
            right = jnp.where(low, pltpu.roll(second, 124, 1), first)
            send_e[a, 0, rows, :] = jnp.where(i_odd, left, right)
            send_o[a, 0, rows, :] = jnp.where(i_odd, right, left)
        for g, (a, far) in enumerate(GHOST):
            top, bottom = kept[R - far][a], kept[far - 1][a]
            send_a[g, 0, rows, :] = jnp.where(j_odd, bottom, top)
            send_b[g, 0, rows, :] = jnp.where(j_odd, top, bottom)
        return carry

    lax.fori_loop(0, TILES, tile, 0)


def merged_columns(i_odd, low, recv_e, recv_o, a, rows):
    got_e, got_o = recv_e[a, 0, rows, :], recv_o[a, 0, rows, :]
    left = jnp.where(i_odd, got_o, got_e)
    right = jnp.where(i_odd, got_e, got_o)
    first = jnp.where(low, left, right)
    second = jnp.where(low, pltpu.roll(left, 124, 1), pltpu.roll(right, 4, 1))
    return first, second


def corner_kernel(meta, recv_e, recv_o, corner_a, corner_b):
    i_odd = meta[0] == 1
    j_odd = meta[1] == 1
    lane = lanes()
    slot = slot_of(lane)
    low = (lane & 7) < 4

    def tile(k, carry):
        rows = pl.ds(pl.multiple_of(8 * k, 8), 8)
        merged = [merged_columns(i_odd, low, recv_e, recv_o, a, rows) for a in range(3)]
        top = jnp.zeros((8, C), jnp.float32)
        bottom = jnp.zeros((8, C), jnp.float32)
        for g, (a, far) in enumerate(GHOST):
            top = jnp.where(slot == g, pltpu.roll(merged[a][1], (8 * (g - (16 - far))) % C, 1), top)
            bottom = jnp.where(slot == g, pltpu.roll(merged[a][0], (8 * (g - (far - 1))) % C, 1), bottom)
        corner_a[0, rows, :] = jnp.where(j_odd, bottom, top)
        corner_b[0, rows, :] = jnp.where(j_odd, top, bottom)
        return carry

    lax.fori_loop(0, TILES, tile, 0)


def ring_east(main, halo, last):
    rm, rh = pltpu.roll(main, C - 1, 1), pltpu.roll(halo, C - 1, 1)
    return jnp.where(last, rh, rm), jnp.where(last, rm, rh)


def ring_west(main, halo, first):
    rm, rh = pltpu.roll(main, 1, 1), pltpu.roll(halo, 1, 1)
    return jnp.where(first, rh, rm), jnp.where(first, rm, rh)


def zonal(values, edge, first, last):
    east = ring_east(*values, last)
    flux = tuple(e * (u - n) for e, u, n in zip(edge, values, east))
    west = ring_west(*flux, first)
    return tuple(f - w for f, w in zip(flux, west))


def stream(low_row, high_row, data, emit, first, last):
    both = (0, 1)
    src, edge, vert, one, two = {}, {}, {}, {}, {}
    n1, n2, n3 = {}, {}, {}
    root = {}
    lo, hi = low_row - 3, high_row + 2
    for r in range(lo, hi + 1):
        s, z, m = data(r)
        src[r], root[r] = s, m
        if z is not None:
            east = ring_east(*z, last)
            edge[r] = tuple(z[h] * east[h] for h in both)
        if r == lo:
            continue
        p = r - 1
        vert[p] = tuple(root[p][h] * m[h] for h in both)
        n1[p] = tuple(vert[p][h] * (src[p][h] - src[r][h]) for h in both)
        if p == lo:
            continue
        flux = zonal(src[p], edge[p], first, last)
        one[p] = tuple(
            (B2 - 1.0) * src[p][h] + flux[h] + n1[p][h] - n1[p - 1][h] for h in both
        )
        if p == lo + 1:
            continue
        q = p - 1
        n2[q] = tuple(vert[q][h] * (one[q][h] - one[p][h]) for h in both)
        if q == lo + 1:
            continue
        flux = zonal(one[q], edge[q], first, last)
        two[q] = tuple(
            B1 * src[q][h] - one[q][h] + flux[h] + n2[q][h] - n2[q - 1][h] for h in both
        )
        if q == lo + 2:
            continue
        t = q - 1
        n3[t] = vert[t][0] * (two[t][0] - two[q][0])
        if t == lo + 2:
            continue
        flux = zonal(two[t], edge[t], first, last)
        emit(t, B0 * src[t][0] - two[t][0] + flux[0] + n3[t] - n3[t - 1])


def main_kernel(
    meta, field, diff_i, diff_j, land, mix,
    recv_a, recv_b, recv_c, recv_x, recv_e, recv_o, corner_a, corner_b,
    out, north, south, diffused,
):
    i_odd = meta[0] == 1
    j_odd = meta[1] == 1
    at_top = meta[2] == 3
    at_bottom = meta[2] == 0
    shift = meta[3]
    refs = (field, diff_i, diff_j, land)
    lane = lanes()
    low = (lane & 7) < 4
    first, last = lane == 0, lane == C - 1

    @pl.when(at_top)
    def _():
        index = (shift - lane) & (C - 1)
        inside = lane <= shift
        beyond = ((shift <= 1) & (lane >= C - 2)) | ((shift >= C - 3) & (lane <= 2))

        def tile(k, carry):
            rows = pl.ds(pl.multiple_of(8 * k, 8), 8)
            for g in range(8):
                one, two, three = recv_b[g, 0, rows, :], recv_c[g, 0, rows, :], recv_x[g, 0, rows, :]
                own = jnp.where(inside, one, two)
                other = jnp.where(beyond, three, jnp.where(inside, two, one))
                north[g, 0, rows, :] = jnp.take_along_axis(own, index, axis=1)
                north[g, 1, rows, :] = jnp.take_along_axis(other, index, axis=1)
            return carry

        lax.fori_loop(0, TILES, tile, 0)

    @pl.when(jnp.logical_not(at_top))
    def _():
        def tile(k, carry):
            rows = pl.ds(pl.multiple_of(8 * k, 8), 8)
            corner = jnp.where(j_odd, corner_b[0, rows, :], corner_a[0, rows, :])
            for g in range(8):
                north[g, 0, rows, :] = jnp.where(j_odd, recv_b[g, 0, rows, :], recv_a[g, 0, rows, :])
                north[g, 1, rows, :] = pltpu.roll(corner, (C - 8 * g) % C, 1) if g else corner
            return carry

        lax.fori_loop(0, TILES, tile, 0)

    def south_tile(k, carry):
        rows = pl.ds(pl.multiple_of(8 * k, 8), 8)
        corner = jnp.where(j_odd, corner_a[0, rows, :], corner_b[0, rows, :])
        corner = jnp.where(at_bottom, 0.0, corner)
        for g in range(8):
            got = jnp.where(j_odd, recv_a[g, 0, rows, :], recv_b[g, 0, rows, :])
            south[g, 0, rows, :] = jnp.where(at_bottom, 0.0, got)
            south[g, 1, rows, :] = pltpu.roll(corner, (C - 8 * g) % C, 1) if g else corner
        return carry

    lax.fori_loop(0, TILES, south_tile, 0)

    def tile(k, carry):
        start = tile_start(k)
        rows = pl.ds(pl.multiple_of(8 * k, 8), 8)
        merged = [merged_columns(i_odd, low, recv_e, recv_o, a, rows) for a in range(3)]

        def data(r):
            if 0 <= r < R:
                half, index = divmod(r, 16)
                values = cell(refs, start, r)
                halo = [
                    pltpu.roll(merged[a][half], C - 8 * index, 1) if index else merged[a][half]
                    for a in range(3)
                ]
                return tuple((values[a], halo[a]) for a in range(3))
            ghost, far = (south, -r) if r < 0 else (north, r - R + 1)
            pick = lambda g: (ghost[g, 0, rows, :], ghost[g, 1, rows, :])
            return (pick(far - 1), pick(far + 2) if far <= 2 else None, pick(far + 4))

        def emit(r, value):
            diffused[r, rows, :] = value

        stream(0, R, data, emit, first, last)
        return carry

    lax.fori_loop(0, TILES, tile, 0)

    weights = mix[0]

    def mixing(pair, carry):
        values = jnp.concatenate([diffused[2 * pair], diffused[2 * pair + 1]], axis=1)
        high = values.astype(jnp.bfloat16)
        rest = (values - high.astype(jnp.float32)).astype(jnp.bfloat16)
        stacked = jnp.concatenate([high, rest, high], axis=0)
        result = jnp.dot(weights, stacked, preferred_element_type=jnp.float32)
        for k in range(TILES):
            start = min(8 * k, LAST)
            for side in range(2):
                at = pl.ds(start * R + 2 * pair + side, 8, stride=R)
                wet = land[at, :].astype(jnp.float32)
                out[0, at, :] = result[8 * k : 8 * k + 8, side * C : (side + 1) * C] * wet
        return carry

    lax.fori_loop(0, R // 2, mixing, 0)


def odd_partner(i, count):
    return (((i - 1) % count) ^ 1) + 1


def body(field, diff_i, diff_j, land_sea, partner, vertical):
    count = lax.axis_size("ia")
    ia, ja = lax.axis_index("ia"), lax.axis_index("ja")
    centre = partner[0]
    block, shift = centre // C, centre % C
    meta = jnp.stack([ia % 2, ja % 2, ja, shift]).astype(jnp.int32)

    flat = lambda x: x.reshape(V, L * R, C)
    raw = (flat(field), flat(diff_i), flat(diff_j), land_sea.reshape(L * R, C))
    raw_specs = [pl.BlockSpec((1, L * R, C), lambda v: (v, 0, 0)) for _ in range(3)]
    raw_specs.append(pl.BlockSpec((L * R, C), lambda v: (0, 0)))
    smem = pl.BlockSpec(memory_space=pltpu.SMEM)
    planes = lambda n: jax.ShapeDtypeStruct((n, V, SLOTS, C), jnp.float32)
    plane_spec = lambda n: pl.BlockSpec((n, 1, SLOTS, C), lambda v: (0, v, 0, 0))
    corner_shape = jax.ShapeDtypeStruct((V, SLOTS, C), jnp.float32)
    corner_spec = pl.BlockSpec((1, SLOTS, C), lambda v: (v, 0, 0))

    send_a, send_b, send_e, send_o = pl.pallas_call(
        pack_kernel,
        grid=(V,),
        in_specs=[smem] + raw_specs,
        out_specs=[plane_spec(8), plane_spec(8), plane_spec(3), plane_spec(3)],
        out_shape=[planes(8), planes(8), planes(3), planes(3)],
        compiler_params=pltpu.CompilerParams(vmem_limit_bytes=32 * 2**20),
        name="pack",
    )(meta, *raw)

    both = ("ia", "ja")
    rows_a = [(0, 1), (1, 0), (2, 3), (3, 2)]
    rows_b = [(1, 2), (2, 1)]
    even = [(i, i ^ 1) for i in range(count)]
    odd = [(i, odd_partner(i, count) % count) for i in range(count)]

    def fold_pairs(q):
        return [(t * 4 + 3, ((q - t) % count) * 4 + 3) for t in range(count)]

    def fold_and_rows(q):
        return fold_pairs(q) + [(t * 4 + a, t * 4 + b) for t in range(count) for a, b in rows_b]

    def exchange(q, send_a, send_b, send_e, send_o, meta):
        recv_e = lax.ppermute(send_e, "ia", even)
        recv_o = lax.ppermute(send_o, "ia", odd)
        recv_a = lax.ppermute(send_a, "ja", rows_a)
        recv_b = lax.ppermute(send_b, both, fold_and_rows(q))
        recv_c = lax.ppermute(send_b, both, fold_pairs(q - 1))
        return recv_a, recv_b, recv_c, recv_e, recv_o

    recv_a, recv_b, recv_c, recv_e, recv_o = lax.switch(
        block, [functools.partial(exchange, q) for q in range(count)],
        send_a, send_b, send_e, send_o, meta,
    )
    corner_a, corner_b = pl.pallas_call(
        corner_kernel,
        grid=(V,),
        in_specs=[smem, plane_spec(3), plane_spec(3)],
        out_specs=[corner_spec, corner_spec],
        out_shape=[corner_shape, corner_shape],
        name="corners",
    )(meta, recv_e, recv_o)
    corner_a = lax.ppermute(corner_a, "ja", rows_a)
    corner_b = lax.ppermute(corner_b, "ja", rows_b)

    third = jnp.where(shift <= 1, block + count - 2, block + 1) % count
    recv_x = lax.cond(
        (shift <= 1) | (shift >= C - 3),
        lambda x: lax.switch(
            third,
            [functools.partial(lambda q, y: lax.ppermute(y, both, fold_pairs(q)), q) for q in range(count)],
            x,
        ),
        lambda x: x,
        send_b,
    )

    order = np.array(list(range(8 * (TILES - 1))) + list(range(LAST, L)))
    used = np.ones(SLOTS, np.float32)
    used[8 * (TILES - 1) : 8 * (TILES - 1) + 8 * TILES - L] = 0.0
    mix = vertical[:, order][:, :, order] * (used * np.float32(LEAD))
    high = lax.reduce_precision(mix, 8, 7)
    rest = mix - high
    weights = jnp.concatenate([high, high, rest], axis=2).astype(jnp.bfloat16)

    result = pl.pallas_call(
        main_kernel,
        grid=(V,),
        in_specs=[smem] + raw_specs
        + [pl.BlockSpec((1, SLOTS, 3 * SLOTS), lambda v: (v, 0, 0))]
        + [plane_spec(8)] * 4 + [plane_spec(3)] * 2 + [corner_spec] * 2,
        out_specs=pl.BlockSpec((1, L * R, C), lambda v: (v, 0, 0)),
        out_shape=jax.ShapeDtypeStruct((V, L * R, C), jnp.float32),
        scratch_shapes=[
            pltpu.VMEM((8, 2, SLOTS, C), jnp.float32),
            pltpu.VMEM((8, 2, SLOTS, C), jnp.float32),
            pltpu.VMEM((R, SLOTS, C), jnp.float32),
        ],
        compiler_params=pltpu.CompilerParams(vmem_limit_bytes=48 * 2**20),
        name="diffuse_and_mix",
    )(meta, *raw, weights, recv_a, recv_b, recv_c, recv_x, recv_e, recv_o, corner_a, corner_b)
    return result.reshape(V, L, R, C)


def solution(mesh):
    placed = (
        P(None, None, "ja", "ia"),
        P(None, None, "ja", "ia"),
        P(None, None, "ja", "ia"),
        P(None, "ja", "ia"),
        P(),
        P(),
    )
    return jax.shard_map(
        body, mesh=mesh, in_specs=placed, out_specs=P(None, None, "ja", "ia"), check_vma=False
    )
```

```python
import functools
import numpy as np
import jax
import jax.numpy as jnp
from jax import lax
from jax.experimental import pallas as pl
from jax.experimental.pallas import tpu as pltpu
from jax.sharding import PartitionSpec as P

ITERS = 4
diff_ceiling = 8.0
V, L, R, C = 2, 75, 32, 128
TILES = 10
SLOTS = 8 * TILES
DEPTH = V * SLOTS
CENTRE, HALF = 33.0, 32.0
ROOT_SCALE = 32.0**-0.5


def chebyshev_steps(count):
    lowest_eig = 1.0
    highest_eig = 1.0 + 8.0 * diff_ceiling
    centre_val = 0.5 * (highest_eig + lowest_eig)
    half_width = 0.5 * (highest_eig - lowest_eig)
    plan = []
    step_size = 1.0 / centre_val
    momentum = 0.0
    plan.append((step_size, momentum))
    for turn_index in range(1, count):
        if turn_index == 1:
            momentum = 0.5 * (half_width * step_size) ** 2
        else:
            momentum = (0.5 * half_width * step_size) ** 2
        step_size = 1.0 / (centre_val - momentum / step_size)
        plan.append((step_size, momentum))
    return plan


def polynomial():
    poly = np.polynomial.polynomial
    operator = np.array([CENTRE, HALF])
    iterate = np.zeros(1)
    residual = np.ones(1)
    direction = np.zeros(1)
    for turn_index, (step_size, momentum) in enumerate(chebyshev_steps(ITERS)):
        direction = poly.polyadd(residual, momentum * direction)
        iterate = poly.polyadd(iterate, step_size * direction)
        if turn_index < ITERS - 1:
            residual = poly.polysub(residual, step_size * poly.polymul(operator, direction))
    return [float(c) for c in iterate]


POLY = polynomial()
LEAD = POLY[3]
B2, B1, B0 = POLY[2] / LEAD, POLY[1] / LEAD, POLY[0] / LEAD

GHOST = [(0, 1), (0, 2), (0, 3), (1, 1), (1, 2), (2, 1), (2, 2), (2, 3)]
PLANES = 5


def place(r):
    return divmod(r + 3, PLANES)


def lanes(rows=8):
    return lax.broadcasted_iota(jnp.int32, (rows, C), 1)


def roll(x, by):
    if isinstance(by, int):
        by = by % C
        return pltpu.roll(x, by, 1) if by else x
    return pltpu.roll(x, by & (C - 1), 1)


def slot_of(lane):
    return ((lane + 8) >> 4) & 7


def parities():
    return (lax.axis_index("ia") & 1) == 1, (lax.axis_index("ja") & 1) == 1


def start_rows(raw, kept, sems, spans):
    field, diff_i, diff_j, land = raw
    f, di, dj, ls = kept
    for v in range(V):
        at = pl.ds(v * SLOTS, L)
        for low, count in spans:

            def row(r, carry):
                pltpu.make_async_copy(field.at[v, :, r], f.at[r, at], sems.at[v]).start()
                pltpu.make_async_copy(diff_i.at[v, :, r], di.at[r, at], sems.at[2 + v]).start()
                pltpu.make_async_copy(diff_j.at[v, :, r], dj.at[r, at], sems.at[4 + v]).start()
                return carry

            lax.fori_loop(low, low + count, row, 0)


def start_land(land, ls, sem, spans):
    for low, count in spans:

        def row(r, carry):
            pltpu.make_async_copy(land.at[:, r], ls.at[r, pl.ds(0, L)], sem).start()
            return carry

        lax.fori_loop(low, low + count, row, 0)


def wait_for(ref, sem):
    pltpu.make_async_copy(ref, ref, sem).wait()


def wait_rows(kept, sems, v, count):
    for j in range(3):
        wait_for(kept[j].at[pl.ds(0, count), pl.ds(v * SLOTS, L)], sems.at[2 * j + v])


def root(x):
    return x * lax.rsqrt(x)


def cell(kept, t, k, r):
    f, di, dj, ls = kept
    at = pl.ds(pl.multiple_of(8 * t, 8), 8)
    wet = ls[r, pl.ds(pl.multiple_of(8 * k, 8), 8), :].astype(jnp.float32)
    scaled = wet * ROOT_SCALE
    return f[r, at, :] * wet, root(di[r, at, :]) * scaled, root(dj[r, at, :]) * scaled


RAW_SCRATCH = [
    pltpu.VMEM((R, DEPTH, C), jnp.float32),
    pltpu.VMEM((R, DEPTH, C), jnp.float32),
    pltpu.VMEM((R, DEPTH, C), jnp.float32),
    pltpu.VMEM((R, SLOTS, C), jnp.int32),
    pltpu.SemaphoreType.DMA((7,)),
]
ALL_ROWS = [(0, R)]


def tiles(kept, sems, count, tile):
    def body(t, carry):
        for v in range(V):

            @pl.when(t == v * TILES)
            def _():
                wait_rows(kept, sems, v, count)

        tile(t, lax.rem(t, TILES))
        return carry

    lax.fori_loop(0, DEPTH // 8, body, 0)


EDGE = 6
EDGE_ROWS = [(0, EDGE), (R - EDGE, EDGE)]
OUTER_ROWS = [(0, 3), (R - 3, 3)]


def wait_land(ls, sem, count):
    wait_for(ls.at[pl.ds(0, count), pl.ds(0, L)], sem)


def rows_kernel(field, diff_i, diff_j, land, send_a, send_b, send_x, f, di, dj, ls, sems):
    _, j_odd = parities()
    kept = (f, di, dj, ls)
    start_land(land, ls, sems.at[6], OUTER_ROWS)
    start_rows((field, diff_i, diff_j, land), kept, sems, OUTER_ROWS)
    slot = slot_of(lanes())
    wait_land(ls, sems.at[6], 6)

    def tile(t, k):
        rows = pl.ds(pl.multiple_of(8 * t, 8), 8)
        edge = {r: cell(kept, t, k, r) for r in (0, 1, 2, R - 3, R - 2, R - 1)}
        third = jnp.zeros((8, C), jnp.float32)
        for g, (a, far) in enumerate(GHOST):
            top, bottom = edge[R - far][a], edge[far - 1][a]
            send_a[g, rows, :] = jnp.where(j_odd, bottom, top)
            send_b[g, rows, :] = jnp.where(j_odd, top, bottom)
            third = jnp.where(slot == g, roll(top, 16 * g), third)
        send_x[rows, :] = third

    tiles(kept, sems, 6, tile)


def columns_kernel(
    field, diff_i, diff_j, land, columns_e, columns_o, strips, f, di, dj, ls, sems
):
    i_odd, _ = parities()
    kept = (f, di, dj, ls)
    start_land(land, ls, sems.at[6], ALL_ROWS)
    start_rows((field, diff_i, diff_j, land), kept, sems, ALL_ROWS)
    lane = lanes()
    slot = slot_of(lane)
    in_slot = lane & 15
    wait_land(ls, sems.at[6], R)

    def tile(t, k):
        rows = pl.ds(pl.multiple_of(8 * t, 8), 8)
        packed = [[jnp.zeros((8, C), jnp.float32) for _ in range(PLANES)] for _ in range(3)]
        for r in range(R):
            values = cell(kept, t, k, r)
            index, p = place(r)
            for a in range(3):
                packed[a][p] = jnp.where(slot == index, roll(values[a], 16 * index), packed[a][p])
        for a in range(3):
            left, right = packed[a][0], packed[a][0]
            for p in range(PLANES):
                strips[a, p, rows, :] = packed[a][p]
                if p:
                    left = jnp.where(in_slot >= 3 * p, roll(packed[a][p], 3 * p), left)
                    right = jnp.where(in_slot < 16 - 3 * p, roll(packed[a][p], -3 * p), right)
            columns_e[a, rows, :] = jnp.where(i_odd, left, right)
            columns_o[a, rows, :] = jnp.where(i_odd, right, left)

    tiles(kept, sems, R, tile)


WIDE = 32


def ghost_kernel(columns_e, columns_o, recv_a, recv_b, send_e, send_o):
    i_odd, j_odd = parities()
    lane = lanes(WIDE)

    def tile(t, carry):
        rows = pl.ds(pl.multiple_of(WIDE * t, 8), WIDE)
        for a in range(3):
            got_e, got_o = columns_e[a, rows, :], columns_o[a, rows, :]
            left = jnp.where(i_odd, got_e, got_o)
            right = jnp.where(i_odd, got_o, got_e)
            for g, (b, far) in enumerate(GHOST):
                if a != b:
                    continue
                one, two = recv_a[g, rows, :], recv_b[g, rows, :]
                for r, ghost in ((-far, jnp.where(j_odd, one, two)), (R - 1 + far, jnp.where(j_odd, two, one))):
                    at, p = place(r)
                    by = (16 * at + 3 * p) % C
                    here = (lane >= by) & (lane < by + 3)
                    left = jnp.where(here, roll(ghost, by), left)
                    by = (16 * at - 3 - 3 * p) % C
                    here = (lane >= by) & (lane < by + 3)
                    right = jnp.where(here, roll(ghost, by + 3), right)
            send_e[a, rows, :] = jnp.where(i_odd, left, right)
            send_o[a, rows, :] = jnp.where(i_odd, right, left)
        return carry

    lax.fori_loop(0, DEPTH // WIDE, tile, 0)


def zonal(u, edge):
    flux = edge * (u - roll(u, -1))
    return flux - roll(flux, 1)


def stream(low_row, high_row, data, emit, not_last):
    src, root_j, edge, vert, one, two = {}, {}, {}, {}, {}, {}
    n1, n2, n3 = {}, {}, {}
    lo, hi = low_row - 3, high_row + 2
    for r in range(lo, hi + 1):
        src[r], z, root_j[r] = data(r)
        if z is not None:
            edge[r] = z * not_last * roll(z, -1)
        if r == lo:
            continue
        p = r - 1
        vert[p] = root_j[p] * root_j[r]
        n1[p] = vert[p] * (src[p] - src[r])
        if p == lo:
            continue
        one[p] = (B2 - 1.0) * src[p] + zonal(src[p], edge[p]) + n1[p] - n1[p - 1]
        if p == lo + 1:
            continue
        q = p - 1
        n2[q] = vert[q] * (one[q] - one[p])
        if q == lo + 1:
            continue
        two[q] = B1 * src[q] - one[q] + zonal(one[q], edge[q]) + n2[q] - n2[q - 1]
        if q == lo + 2:
            continue
        t = q - 1
        n3[t] = vert[t] * (two[t] - two[q])
        if t == lo + 2:
            continue
        emit(t, B0 * src[t] - two[t] + zonal(two[t], edge[t]) + n3[t] - n3[t - 1])


def strip_rows(src, z, m):
    after = lambda x: [x[p + 1] if p + 1 < PLANES else roll(x[0], -16) for p in range(PLANES)]
    before = lambda x: [x[p - 1] if p else roll(x[PLANES - 1], 16) for p in range(PLANES)]
    edge = [x * roll(x, -1) for x in z]
    vert = [x * y for x, y in zip(m, after(m))]

    def apply(u, base):
        flux = [c * (x - y) for c, x, y in zip(vert, u, after(u))]
        return [
            b + zonal(x, e) + f - g
            for b, x, e, f, g in zip(base, u, edge, flux, before(flux))
        ]

    one = apply(src, [(B2 - 1.0) * s for s in src])
    two = apply(one, [B1 * s - u for s, u in zip(src, one)])
    return apply(two, [B0 * s - u for s, u in zip(src, two)])


def inner_kernel(field, diff_i, diff_j, land, out, f, di, dj, ls, sems):
    kept = (f, di, dj, ls)
    start_land(land, ls, sems.at[6], ALL_ROWS)
    start_rows((field, diff_i, diff_j, land), kept, sems, ALL_ROWS)
    not_last = jnp.where(lanes() == C - 1, 0.0, 1.0)
    wait_for(ls.at[:, pl.ds(0, L)], sems.at[6])

    def tile(t, k):
        def emit(r, value):
            out[r - 3, pl.ds(pl.multiple_of(8 * t, 8), 8), :] = value

        stream(3, R - 3, lambda r: cell(kept, t, k, r), emit, not_last)

    tiles(kept, sems, R, tile)


def finish_kernel(
    partner, field, diff_i, diff_j, land, inner, mix, strips,
    recv_a, recv_b, near, far, recv_e, recv_o, recv_x,
    out, north, south, north_halo, east, west, fold, diffused, mixed,
    f, di, dj, ls, sems, got, out_sem,
):
    i_odd, j_odd = parities()
    at_top = lax.axis_index("ja") == 3
    at_bottom = lax.axis_index("ja") == 0
    shift = partner[0] & (C - 1)
    kept = (f, di, dj, ls)
    start_land(land, ls, sems.at[6], ALL_ROWS)
    start_rows((field, diff_i, diff_j, land), kept, sems, EDGE_ROWS)

    def choose(flag, first, second, to, sem):
        @pl.when(flag)
        def _():
            pltpu.make_async_copy(first, to, sem).start()

        @pl.when(jnp.logical_not(flag))
        def _():
            pltpu.make_async_copy(second, to, sem).start()

    choose(i_odd, recv_o, recv_e, east, got.at[0])
    choose(i_odd, recv_e, recv_o, west, got.at[1])
    choose(j_odd, recv_a, recv_b, south, got.at[3])

    @pl.when(at_top)
    def _():
        pltpu.make_async_copy(near, north, got.at[2]).start()

    @pl.when(jnp.logical_not(at_top))
    def _():
        choose(j_odd, recv_b, recv_a, north, got.at[2])

    fold_copy = pltpu.make_async_copy(far, fold, got.at[4])
    fold_copy.start()
    inner_copy = pltpu.make_async_copy(inner, diffused.at[pl.ds(3, R - 6)], got.at[5])
    inner_copy.start()
    for j, ref in enumerate((east, west, north, south)):
        wait_for(ref, got.at[j])
    fold_copy.wait()

    wide = lanes(DEPTH)
    wide_slot = slot_of(wide)

    @pl.when(at_top)
    def _():
        index = (shift - wide) & (C - 1)
        inside = wide <= shift
        beyond = ((shift <= 1) & (wide >= C - 2)) | ((shift >= C - 3) & (wide <= 2))

        def ghost(g, carry):
            one, two, three = north[g], fold[g], roll(recv_x[...], -16 * g)
            own = jnp.where(inside, one, two)
            other = jnp.where(beyond, three, jnp.where(inside, two, one))
            north[g] = jnp.take_along_axis(own, index, axis=1)
            other = roll(jnp.take_along_axis(other, index, axis=1), 16 * g)
            north_halo[...] = jnp.where(wide_slot == g, other, north_halo[...])
            return carry

        lax.fori_loop(0, 8, ghost, 0)

    @pl.when(at_bottom)
    def _():
        south[...] = jnp.zeros_like(south)

    lane = lanes()
    in_slot = lane & 15
    slot = slot_of(lane)
    not_last = jnp.where(lane == C - 1, 0.0, 1.0)
    seam = (lane < 3) | (lane >= C - 3)
    sublane = lax.broadcasted_iota(jnp.int32, (8, C), 0)
    zero = jnp.zeros((8, C), jnp.float32)
    wait_for(ls.at[:, pl.ds(0, L)], sems.at[6])
    inner_copy.wait()

    def tile(t, k):
        rows = pl.ds(pl.multiple_of(8 * t, 8), 8)
        real = 8 * k + sublane < L

        def ghost(r):
            planes, far = (south, -r) if r < 0 else (north, r - R + 1)
            pick = lambda g: planes[g, rows, :]
            return (pick(far - 1), pick(far + 2) if far <= 2 else None, pick(far + 4))

        left = [[None] * PLANES for _ in range(3)]
        right = [[None] * PLANES for _ in range(3)]
        for a in range(3):
            got_east, got_west = east[a, rows, :], west[a, rows, :]
            for p in range(PLANES):
                own = strips[a, p, rows, :]
                halo = jnp.where(in_slot < 8, roll(got_east, -3 * p), roll(got_west, 3 * p))
                for r in (-3, -2, -1, R, R + 1, R + 2):
                    at, plane = place(r)
                    if plane != p:
                        continue
                    far = -r if r < 0 else r - R + 1
                    mine, theirs = zero, zero
                    if (a, far) in GHOST:
                        g = GHOST.index((a, far))
                        mine = roll((south if r < 0 else north)[g, rows, :], 16 * at)
                        theirs = roll(north_halo[rows, :], 16 * (at - g))
                    here = slot == at
                    own = jnp.where(here, mine, own)
                    if r >= R:
                        halo = jnp.where(here & at_top, theirs, halo)
                left[a][p] = jnp.where(in_slot >= 13, halo, own)
                right[a][p] = jnp.where(in_slot < 3, halo, own)
        left = strip_rows(*left)
        right = strip_rows(*right)
        fixed = [jnp.where(in_slot < 8, x, y) for x, y in zip(left, right)]

        def emit(r, value):
            at, p = place(r)
            value = jnp.where(seam, roll(fixed[p], -16 * at), value)
            diffused[r, rows, :] = jnp.where(real, value, 0.0)

        data = lambda r: cell(kept, t, k, r) if 0 <= r < R else ghost(r)
        stream(0, 3, data, emit, not_last)
        stream(R - 3, R, data, emit, not_last)
        for r in range(3, R - 3):
            emit(r, diffused[r, rows, :])

    tiles(kept, sems, 2 * EDGE, tile)

    for v in range(V):
        at = pl.ds(v * SLOTS, SLOTS)

        def pair_of_rows(pair, carry):
            values = jnp.concatenate([diffused[2 * pair, at], diffused[2 * pair + 1, at]], axis=1)
            high = values.astype(jnp.bfloat16)
            rest = (values - high.astype(jnp.float32)).astype(jnp.bfloat16)
            stacked = jnp.concatenate([high, rest, high], axis=0)
            result = jnp.dot(mix[v], stacked, preferred_element_type=jnp.float32)
            for side in range(2):
                r = 2 * pair + side
                mixed[r, at] = result[:, side * C : (side + 1) * C] * ls[r].astype(jnp.float32)
                pltpu.make_async_copy(mixed.at[r, pl.ds(v * SLOTS, L)], out.at[v, :, r], out_sem.at[v]).start()
            return carry

        lax.fori_loop(0, R // 2, pair_of_rows, 0, unroll=2)

    for v in range(V):
        wait_for(mixed.at[:, pl.ds(v * SLOTS, L)], out_sem.at[v])


def odd_partner(i, count):
    return (((i - 1) % count) ^ 1) + 1


def body(field, diff_i, diff_j, land_sea, partner, vertical):
    count = lax.axis_size("ia")
    raw = (field, diff_i, diff_j, land_sea)
    hbm = pl.BlockSpec(memory_space=pltpu.HBM)
    vmem = pl.BlockSpec(memory_space=pltpu.VMEM)
    planes = lambda *n: jax.ShapeDtypeStruct(n + (DEPTH, C), jnp.float32)
    scratch = lambda *n: pltpu.VMEM(n + (DEPTH, C), jnp.float32)
    big = pltpu.CompilerParams(vmem_limit_bytes=48 * 2**20)

    def cost(flops, size):
        return pl.CostEstimate(flops=flops, bytes_accessed=size, transcendentals=0)

    send_a, send_b, send_x = pl.pallas_call(
        rows_kernel,
        in_specs=[hbm] * 4,
        out_specs=[vmem] * 3,
        out_shape=[planes(8), planes(8), planes()],
        scratch_shapes=RAW_SCRATCH,
        compiler_params=big,
        name="pack_rows",
    )(*raw)
    columns_e, columns_o, strips = pl.pallas_call(
        columns_kernel,
        in_specs=[hbm] * 4,
        out_specs=[vmem] * 3,
        out_shape=[planes(3), planes(3), planes(3, PLANES)],
        scratch_shapes=RAW_SCRATCH,
        compiler_params=big,
        cost_estimate=cost(10**8, 16 * 10**6),
        name="pack_columns",
    )(*raw)

    both = ("ia", "ja")
    rows_a = [(0, 1), (1, 0), (2, 3), (3, 2)]
    rows_b = [(1, 2), (2, 1)]
    even = [(i, i ^ 1) for i in range(count)]
    odd = [(i, odd_partner(i, count) % count) for i in range(count)]

    def fold(q):
        return [(t * 4 + 3, ((q - t) % count) * 4 + 3) for t in range(count)]

    centre = partner[0]
    block, shift = lax.shift_right_logical(centre, 7), centre & (C - 1)

    def mirror(x, q):
        return lax.ppermute(x, both, fold(q))

    def third_block(x):
        turn = jnp.where(shift <= 1, block - 2, block + 1)
        x = mirror(x, 0)
        for bit in range((count - 1).bit_length()):
            rotate = functools.partial(lambda y, step: mirror(mirror(y, 0), step), step=2**bit)
            x = lax.cond((turn >> bit) & 1 == 1, rotate, lambda y: y, x)
        return x

    recv_x = lax.cond((shift <= 1) | (shift >= C - 3), third_block, lambda x: x, send_x)

    mix = jnp.pad(vertical * np.float32(LEAD), ((0, 0), (0, SLOTS - L), (0, SLOTS - L)))
    high = lax.reduce_precision(mix, 8, 7)
    weights = jnp.concatenate([high, high, mix - high], axis=2).astype(jnp.bfloat16)

    recv_a = lax.ppermute(send_a, "ja", rows_a)
    recv_b = lax.ppermute(send_b, "ja", rows_b)
    send_e, send_o = pl.pallas_call(
        ghost_kernel,
        in_specs=[vmem] * 4,
        out_specs=[vmem] * 2,
        out_shape=[planes(3), planes(3)],
        name="pack_ghost_columns",
    )(columns_e, columns_o, recv_a, recv_b)
    recv_e = lax.ppermute(send_e, "ia", even)
    recv_o = lax.ppermute(send_o, "ia", odd)

    def fold_and_inner(q, send_b, raw):
        near = lax.ppermute(send_b, both, fold(q))
        far = lax.ppermute(send_b, both, fold((q - 1) % count))
        inner = pl.pallas_call(
            inner_kernel,
            in_specs=[hbm] * 4,
            out_specs=vmem,
            out_shape=planes(R - 6),
            scratch_shapes=RAW_SCRATCH,
            compiler_params=big,
            cost_estimate=cost(2 * 10**8, 16 * 10**6),
            name="inner",
        )(*raw)
        return near, far, inner

    near, far, inner = lax.switch(
        block, [functools.partial(fold_and_inner, q) for q in range(count)], send_b, raw
    )
    return pl.pallas_call(
        finish_kernel,
        in_specs=[pl.BlockSpec(memory_space=pltpu.SMEM)] + [hbm] * 5 + [vmem] * 2 + [hbm] * 6 + [vmem],
        out_specs=hbm,
        out_shape=jax.ShapeDtypeStruct((V, L, R, C), jnp.float32),
        scratch_shapes=[
            scratch(8), scratch(8), scratch(), scratch(3), scratch(3), scratch(8),
            scratch(R), scratch(R),
        ] + RAW_SCRATCH + [pltpu.SemaphoreType.DMA((6,)), pltpu.SemaphoreType.DMA((V,))],
        compiler_params=big,
        name="finish",
    )(
        partner, *raw, inner, weights, strips,
        recv_a, recv_b, near, far, recv_e, recv_o, recv_x,
    )


def solution(mesh):
    placed = (
        P(None, None, "ja", "ia"),
        P(None, None, "ja", "ia"),
        P(None, None, "ja", "ia"),
        P(None, "ja", "ia"),
        P(),
        P(),
    )
    return jax.shard_map(
        body, mesh=mesh, in_specs=placed, out_specs=P(None, None, "ja", "ia"), check_vma=False
    )
```

```python
import functools
import numpy as np
import jax
import jax.numpy as jnp
from jax import lax
from jax.experimental import pallas as pl
from jax.experimental.pallas import tpu as pltpu
from jax.sharding import PartitionSpec as P

ITERS = 4
diff_ceiling = 8.0
V, L, R, C = 2, 75, 32, 128
SLOTS = 80
DEPTH = V * SLOTS
CENTRE, HALF = 33.0, 32.0
ROOT_SCALE = 32.0**-0.5


def chebyshev_steps(count):
    lowest_eig = 1.0
    highest_eig = 1.0 + 8.0 * diff_ceiling
    centre_val = 0.5 * (highest_eig + lowest_eig)
    half_width = 0.5 * (highest_eig - lowest_eig)
    plan = []
    step_size = 1.0 / centre_val
    momentum = 0.0
    plan.append((step_size, momentum))
    for turn_index in range(1, count):
        if turn_index == 1:
            momentum = 0.5 * (half_width * step_size) ** 2
        else:
            momentum = (0.5 * half_width * step_size) ** 2
        step_size = 1.0 / (centre_val - momentum / step_size)
        plan.append((step_size, momentum))
    return plan


def polynomial():
    poly = np.polynomial.polynomial
    operator = np.array([CENTRE, HALF])
    iterate = np.zeros(1)
    residual = np.ones(1)
    direction = np.zeros(1)
    for turn_index, (step_size, momentum) in enumerate(chebyshev_steps(ITERS)):
        direction = poly.polyadd(residual, momentum * direction)
        iterate = poly.polyadd(iterate, step_size * direction)
        if turn_index < ITERS - 1:
            residual = poly.polysub(residual, step_size * poly.polymul(operator, direction))
    return [float(c) for c in iterate]


POLY = polynomial()
LEAD = POLY[3]
B2, B1, B0 = POLY[2] / LEAD, POLY[1] / LEAD, POLY[0] / LEAD

GHOST = [(0, 1), (0, 2), (0, 3), (1, 1), (1, 2), (2, 1), (2, 2), (2, 3)]
PLANES = 5


def place(r):
    return divmod(r + 3, PLANES)


def lanes(rows):
    return lax.broadcasted_iota(jnp.int32, (rows, C), 1)


def roll(x, by):
    if isinstance(by, int):
        by = by % C
        return pltpu.roll(x, by, 1) if by else x
    return pltpu.roll(x, by & (C - 1), 1)


def slot_of(lane):
    return ((lane + 8) >> 4) & 7


def parities():
    return (lax.axis_index("ia") & 1) == 1, (lax.axis_index("ja") & 1) == 1


def start_rows(raw, kept, sems, spans):
    field, diff_i, diff_j, land = raw
    f, di, dj, ls = kept
    for v in range(V):
        at = pl.ds(v * SLOTS, L)
        for low, count in spans:

            def row(r, carry):
                pltpu.make_async_copy(field.at[v, :, r], f.at[r, at], sems.at[v]).start()
                pltpu.make_async_copy(diff_i.at[v, :, r], di.at[r, at], sems.at[2 + v]).start()
                pltpu.make_async_copy(diff_j.at[v, :, r], dj.at[r, at], sems.at[4 + v]).start()
                return carry

            lax.fori_loop(low, low + count, row, 0)


def start_land(land, ls, sem, spans):
    for low, count in spans:

        def row(r, carry):
            pltpu.make_async_copy(land.at[:, r], ls.at[r, pl.ds(0, L)], sem).start()
            return carry

        lax.fori_loop(low, low + count, row, 0)


def wait_for(ref, sem):
    pltpu.make_async_copy(ref, ref, sem).wait()


def wait_rows(kept, sems, v, count):
    for j in range(3):
        wait_for(kept[j].at[pl.ds(0, count), pl.ds(v * SLOTS, L)], sems.at[2 * j + v])


def root(x):
    return x * lax.rsqrt(x)


def span(tall, t):
    return pl.ds(pl.multiple_of(tall * t, 8), tall)


def cell(kept, tall, t, r):
    f, di, dj, ls = kept
    at = span(tall, t)
    wet = ls[r, span(tall, lax.rem(t, SLOTS // tall)), :].astype(jnp.float32)
    scaled = wet * ROOT_SCALE
    return f[r, at, :] * wet, root(di[r, at, :]) * scaled, root(dj[r, at, :]) * scaled


RAW_SCRATCH = [
    pltpu.VMEM((R, DEPTH, C), jnp.float32),
    pltpu.VMEM((R, DEPTH, C), jnp.float32),
    pltpu.VMEM((R, DEPTH, C), jnp.float32),
    pltpu.VMEM((R, SLOTS, C), jnp.int32),
    pltpu.SemaphoreType.DMA((7,)),
]
ALL_ROWS = [(0, R)]


def tiles(kept, sems, count, tall, tile):
    def body(t, carry):
        for v in range(V):

            @pl.when(t == v * (SLOTS // tall))
            def _():
                wait_rows(kept, sems, v, count)

        tile(t)
        return carry

    lax.fori_loop(0, DEPTH // tall, body, 0)


EDGE = 6
EDGE_ROWS = [(0, EDGE), (R - EDGE, EDGE)]
OUTER_ROWS = [(0, 3), (R - 3, 3)]


def wait_land(ls, sem, count):
    wait_for(ls.at[pl.ds(0, count), pl.ds(0, L)], sem)


ROWS_TALL = 40
COLUMNS_TALL = 40


def rows_kernel(field, diff_i, diff_j, land, send_a, send_b, send_x, f, di, dj, ls, sems):
    _, j_odd = parities()
    kept = (f, di, dj, ls)
    start_land(land, ls, sems.at[6], OUTER_ROWS)
    start_rows((field, diff_i, diff_j, land), kept, sems, OUTER_ROWS)
    slot = slot_of(lanes(ROWS_TALL))
    wait_land(ls, sems.at[6], 6)

    def tile(t):
        rows = span(ROWS_TALL, t)
        edge = {r: cell(kept, ROWS_TALL, t, r) for r in (0, 1, 2, R - 3, R - 2, R - 1)}
        third = jnp.zeros((ROWS_TALL, C), jnp.float32)
        for g, (a, far) in enumerate(GHOST):
            top, bottom = edge[R - far][a], edge[far - 1][a]
            send_a[g, rows, :] = jnp.where(j_odd, bottom, top)
            send_b[g, rows, :] = jnp.where(j_odd, top, bottom)
            third = jnp.where(slot == g, roll(top, 16 * g), third)
        send_x[rows, :] = third

    tiles(kept, sems, 6, ROWS_TALL, tile)


def columns_kernel(
    field, diff_i, diff_j, land, columns_e, columns_o, strips, f, di, dj, ls, sems
):
    i_odd, _ = parities()
    kept = (f, di, dj, ls)
    start_land(land, ls, sems.at[6], ALL_ROWS)
    start_rows((field, diff_i, diff_j, land), kept, sems, ALL_ROWS)
    lane = lanes(COLUMNS_TALL)
    slot = slot_of(lane)
    in_slot = lane & 15
    wait_land(ls, sems.at[6], R)

    def tile(t):
        rows = span(COLUMNS_TALL, t)
        packed = [[jnp.zeros((COLUMNS_TALL, C), jnp.float32) for _ in range(PLANES)] for _ in range(3)]
        for r in range(R):
            values = cell(kept, COLUMNS_TALL, t, r)
            index, p = place(r)
            for a in range(3):
                packed[a][p] = jnp.where(slot == index, roll(values[a], 16 * index), packed[a][p])
        for a in range(3):
            left, right = packed[a][0], packed[a][0]
            for p in range(PLANES):
                strips[a, p, rows, :] = packed[a][p]
                if p:
                    left = jnp.where(in_slot >= 3 * p, roll(packed[a][p], 3 * p), left)
                    right = jnp.where(in_slot < 16 - 3 * p, roll(packed[a][p], -3 * p), right)
            columns_e[a, rows, :] = jnp.where(i_odd, left, right)
            columns_o[a, rows, :] = jnp.where(i_odd, right, left)

    tiles(kept, sems, R, COLUMNS_TALL, tile)


WIDE = 80


def ghost_kernel(columns_e, columns_o, recv_a, recv_b, send_e, send_o):
    i_odd, j_odd = parities()
    lane = lanes(WIDE)

    def tile(t, carry):
        rows = pl.ds(pl.multiple_of(WIDE * t, 8), WIDE)
        for a in range(3):
            got_e, got_o = columns_e[a, rows, :], columns_o[a, rows, :]
            left = jnp.where(i_odd, got_e, got_o)
            right = jnp.where(i_odd, got_o, got_e)
            for g, (b, far) in enumerate(GHOST):
                if a != b:
                    continue
                one, two = recv_a[g, rows, :], recv_b[g, rows, :]
                for r, ghost in ((-far, jnp.where(j_odd, one, two)), (R - 1 + far, jnp.where(j_odd, two, one))):
                    at, p = place(r)
                    by = (16 * at + 3 * p) % C
                    here = (lane >= by) & (lane < by + 3)
                    left = jnp.where(here, roll(ghost, by), left)
                    by = (16 * at - 3 - 3 * p) % C
                    here = (lane >= by) & (lane < by + 3)
                    right = jnp.where(here, roll(ghost, by + 3), right)
            send_e[a, rows, :] = jnp.where(i_odd, left, right)
            send_o[a, rows, :] = jnp.where(i_odd, right, left)
        return carry

    lax.fori_loop(0, DEPTH // WIDE, tile, 0)


def zonal(u, edge):
    flux = edge * (u - roll(u, -1))
    return flux - roll(flux, 1)


def stream(low_row, high_row, data, emit, not_last):
    src, root_j, edge, vert, one, two = {}, {}, {}, {}, {}, {}
    n1, n2, n3 = {}, {}, {}
    lo, hi = low_row - 3, high_row + 2
    for r in range(lo, hi + 1):
        src[r], z, root_j[r] = data(r)
        if z is not None:
            edge[r] = z * not_last * roll(z, -1)
        if r == lo:
            continue
        p = r - 1
        vert[p] = root_j[p] * root_j[r]
        n1[p] = vert[p] * (src[p] - src[r])
        if p == lo:
            continue
        one[p] = (B2 - 1.0) * src[p] + zonal(src[p], edge[p]) + n1[p] - n1[p - 1]
        if p == lo + 1:
            continue
        q = p - 1
        n2[q] = vert[q] * (one[q] - one[p])
        if q == lo + 1:
            continue
        two[q] = B1 * src[q] - one[q] + zonal(one[q], edge[q]) + n2[q] - n2[q - 1]
        if q == lo + 2:
            continue
        t = q - 1
        n3[t] = vert[t] * (two[t] - two[q])
        if t == lo + 2:
            continue
        emit(t, B0 * src[t] - two[t] + zonal(two[t], edge[t]) + n3[t] - n3[t - 1])


def strip_rows(src, z, m):
    after = lambda x: [x[p + 1] if p + 1 < PLANES else roll(x[0], -16) for p in range(PLANES)]
    before = lambda x: [x[p - 1] if p else roll(x[PLANES - 1], 16) for p in range(PLANES)]
    edge = [x * roll(x, -1) for x in z]
    vert = [x * y for x, y in zip(m, after(m))]

    def apply(u, base):
        flux = [c * (x - y) for c, x, y in zip(vert, u, after(u))]
        return [
            b + zonal(x, e) + f - g
            for b, x, e, f, g in zip(base, u, edge, flux, before(flux))
        ]

    one = apply(src, [(B2 - 1.0) * s for s in src])
    two = apply(one, [B1 * s - u for s, u in zip(src, one)])
    return apply(two, [B0 * s - u for s, u in zip(src, two)])


INNER_TALL = 8


def inner_kernel(field, diff_i, diff_j, land, out, f, di, dj, ls, sems):
    kept = (f, di, dj, ls)
    start_land(land, ls, sems.at[6], ALL_ROWS)
    start_rows((field, diff_i, diff_j, land), kept, sems, ALL_ROWS)
    not_last = jnp.where(lanes(INNER_TALL) == C - 1, 0.0, 1.0)
    wait_for(ls.at[:, pl.ds(0, L)], sems.at[6])

    def tile(t):
        def emit(r, value):
            out[r - 3, span(INNER_TALL, t), :] = value

        stream(3, R - 3, lambda r: cell(kept, INNER_TALL, t, r), emit, not_last)

    tiles(kept, sems, R, INNER_TALL, tile)


STRIP_TALL = 40
EDGE_TALL = 40


def finish_kernel(
    partner, field, diff_i, diff_j, land, inner, vertical, strips,
    recv_a, recv_b, near, far, recv_e, recv_o, recv_x,
    out, north, south, north_halo, east, west, fold, own_strips, fixed, diffused, mixed, square, weights,
    f, di, dj, ls, sems, got, out_sem,
):
    i_odd, j_odd = parities()
    at_top = lax.axis_index("ja") == 3
    at_bottom = lax.axis_index("ja") == 0
    shift = partner[0] & (C - 1)
    kept = (f, di, dj, ls)

    def choose(flag, first, second, to, sem):
        @pl.when(flag)
        def _():
            pltpu.make_async_copy(first, to, sem).start()

        @pl.when(jnp.logical_not(flag))
        def _():
            pltpu.make_async_copy(second, to, sem).start()

    choose(i_odd, recv_o, recv_e, east, got.at[0])
    choose(i_odd, recv_e, recv_o, west, got.at[1])
    choose(j_odd, recv_a, recv_b, south, got.at[3])

    @pl.when(at_top)
    def _():
        pltpu.make_async_copy(near, north, got.at[2]).start()
        pltpu.make_async_copy(far, fold, got.at[4]).start()

    @pl.when(jnp.logical_not(at_top))
    def _():
        choose(j_odd, recv_b, recv_a, north, got.at[2])

    strips_copy = pltpu.make_async_copy(strips, own_strips, got.at[6])
    strips_copy.start()
    start_rows((field, diff_i, diff_j, land), kept, sems, EDGE_ROWS)
    start_land(land, ls, sems.at[6], ALL_ROWS)
    inner_copy = pltpu.make_async_copy(inner, diffused.at[pl.ds(3, R - 6)], got.at[5])
    inner_copy.start()

    square[...] = jnp.zeros_like(square)
    for v in range(V):
        square[v, pl.ds(0, L), pl.ds(0, L)] = vertical[:, v, :] * np.float32(LEAD)
        high = square[v].astype(jnp.bfloat16).astype(jnp.float32)
        rest = square[v] - high
        pad = jnp.zeros_like(high)
        high = jnp.concatenate([high, pad], axis=1)
        rest = jnp.concatenate([rest, pad], axis=1)
        both = high + pltpu.roll(high, SLOTS, 1) + pltpu.roll(rest, 2 * SLOTS, 1)
        weights[v] = both.astype(jnp.bfloat16)

    for j, ref in enumerate((east, west, north, south)):
        wait_for(ref, got.at[j])

    @pl.when(at_top)
    def _():
        wait_for(fold, got.at[4])
        wide = lanes(DEPTH)
        wide_slot = slot_of(wide)
        index = (shift - wide) & (C - 1)
        inside = wide <= shift
        beyond = ((shift <= 1) & (wide >= C - 2)) | ((shift >= C - 3) & (wide <= 2))

        def ghost(g, carry):
            one, two, three = north[g], fold[g], roll(recv_x[...], -16 * g)
            own = jnp.where(inside, one, two)
            other = jnp.where(beyond, three, jnp.where(inside, two, one))
            north[g] = jnp.take_along_axis(own, index, axis=1)
            other = roll(jnp.take_along_axis(other, index, axis=1), 16 * g)
            north_halo[...] = jnp.where(wide_slot == g, other, north_halo[...])
            return carry

        lax.fori_loop(0, 8, ghost, 0)

    @pl.when(at_bottom)
    def _():
        south[...] = jnp.zeros_like(south)

    strips_copy.wait()
    lane = lanes(STRIP_TALL)
    in_slot = lane & 15
    slot = slot_of(lane)
    zero = jnp.zeros((STRIP_TALL, C), jnp.float32)

    def strip_tile(n, carry):
        t, side = n >> 1, n & 1
        rows = span(STRIP_TALL, t)
        outside = ((side == 0) & (in_slot >= 13)) | ((side == 1) & (in_slot < 3))
        packed = [[None] * PLANES for _ in range(3)]
        for a in range(3):
            got_east, got_west = east[a, rows, :], west[a, rows, :]
            for p in range(PLANES):
                own = own_strips[a, p, rows, :]
                halo = jnp.where(in_slot < 8, roll(got_east, -3 * p), roll(got_west, 3 * p))
                for r in (-3, -2, -1, R, R + 1, R + 2):
                    at, plane = place(r)
                    if plane != p:
                        continue
                    far_off = -r if r < 0 else r - R + 1
                    mine, theirs = zero, zero
                    if (a, far_off) in GHOST:
                        g = GHOST.index((a, far_off))
                        mine = roll((south if r < 0 else north)[g, rows, :], 16 * at)
                        theirs = roll(north_halo[rows, :], 16 * (at - g))
                    here = slot == at
                    own = jnp.where(here, mine, own)
                    if r >= R:
                        halo = jnp.where(here & at_top, theirs, halo)
                packed[a][p] = jnp.where(outside, halo, own)
        for p, value in enumerate(strip_rows(*packed)):
            fixed[side, p, rows, :] = value
        return carry

    lax.fori_loop(0, 2 * (DEPTH // STRIP_TALL), strip_tile, 0)

    not_last = jnp.where(lanes(EDGE_TALL) == C - 1, 0.0, 1.0)
    wait_land(ls, sems.at[6], R)

    def edge_tile(t, low):
        rows = span(EDGE_TALL, t)

        def ghost(r):
            planes, far_off = (south, -r) if r < 0 else (north, r - R + 1)
            pick = lambda g: planes[g, rows, :]
            return (pick(far_off - 1), pick(far_off + 2) if far_off <= 2 else None, pick(far_off + 4))

        def emit(r, value):
            diffused[r, rows, :] = value

        data = lambda r: cell(kept, EDGE_TALL, t, r) if 0 <= r < R else ghost(r)
        stream(low, low + 3, data, emit, not_last)

    tiles(kept, sems, 2 * EDGE, EDGE_TALL, lambda t: edge_tile(t, 0))

    def upper(t, carry):
        edge_tile(t, R - 3)
        return carry

    lax.fori_loop(0, DEPTH // EDGE_TALL, upper, 0)
    inner_copy.wait()

    wide = lanes(SLOTS)
    from_left = (wide & 15) < 8
    seam = (wide < 3) | (wide >= C - 3)
    real = lax.broadcasted_iota(jnp.int32, (SLOTS, C), 0) < L
    tail = jnp.zeros((2 * C - 3 * SLOTS, 2 * C), jnp.bfloat16)

    for v in range(V):
        at = pl.ds(v * SLOTS, SLOTS)

        def pair_of_rows(pair, carry):
            halves = []
            for side in range(2):
                r = 2 * pair + side
                place_of = lax.div(r + 3, PLANES)
                p = r + 3 - PLANES * place_of
                columns = roll(jnp.where(from_left, fixed[0, p, at], fixed[1, p, at]), -16 * place_of)
                halves.append(jnp.where(real, jnp.where(seam, columns, diffused[r, at]), 0.0))
            values = jnp.concatenate(halves, axis=1)
            high = values.astype(jnp.bfloat16)
            rest = (values - high.astype(jnp.float32)).astype(jnp.bfloat16)
            stacked = jnp.concatenate([high, rest, high, tail], axis=0)
            result = jnp.dot(weights[v], stacked, preferred_element_type=jnp.float32)
            for side in range(2):
                r = 2 * pair + side
                mixed[r, at] = result[:, side * C : (side + 1) * C] * ls[r].astype(jnp.float32)
                pltpu.make_async_copy(mixed.at[r, pl.ds(v * SLOTS, L)], out.at[v, :, r], out_sem.at[v]).start()
            return carry

        lax.fori_loop(0, R // 2, pair_of_rows, 0, unroll=2)

    for v in range(V):
        wait_for(mixed.at[:, pl.ds(v * SLOTS, L)], out_sem.at[v])


def odd_partner(i, count):
    return (((i - 1) % count) ^ 1) + 1


def body(field, diff_i, diff_j, land_sea, partner, vertical):
    count = lax.axis_size("ia")
    raw = (field, diff_i, diff_j, land_sea)
    hbm = pl.BlockSpec(memory_space=pltpu.HBM)
    vmem = pl.BlockSpec(memory_space=pltpu.VMEM)
    planes = lambda *n: jax.ShapeDtypeStruct(n + (DEPTH, C), jnp.float32)
    scratch = lambda *n: pltpu.VMEM(n + (DEPTH, C), jnp.float32)
    big = pltpu.CompilerParams(vmem_limit_bytes=60 * 2**20)

    def cost(flops, size):
        return pl.CostEstimate(flops=flops, bytes_accessed=size, transcendentals=0)

    send_a, send_b, send_x = pl.pallas_call(
        rows_kernel,
        in_specs=[hbm] * 4,
        out_specs=[vmem] * 3,
        out_shape=[planes(8), planes(8), planes()],
        scratch_shapes=RAW_SCRATCH,
        compiler_params=big,
        name="pack_rows",
    )(*raw)
    columns_e, columns_o, strips = pl.pallas_call(
        columns_kernel,
        in_specs=[hbm] * 4,
        out_specs=[vmem] * 3,
        out_shape=[planes(3), planes(3), planes(3, PLANES)],
        scratch_shapes=RAW_SCRATCH,
        compiler_params=big,
        cost_estimate=cost(10**8, 16 * 10**6),
        name="pack_columns",
    )(*raw)

    both = ("ia", "ja")
    rows_a = [(0, 1), (1, 0), (2, 3), (3, 2)]
    rows_b = [(1, 2), (2, 1)]
    even = [(i, i ^ 1) for i in range(count)]
    odd = [(i, odd_partner(i, count) % count) for i in range(count)]

    def fold(q):
        return [(t * 4 + 3, ((q - t) % count) * 4 + 3) for t in range(count)]

    centre = partner[0]
    block, shift = lax.shift_right_logical(centre, 7), centre & (C - 1)

    def mirror(x, q):
        return lax.ppermute(x, both, fold(q))

    def third_block(x):
        turn = jnp.where(shift <= 1, block - 2, block + 1)
        x = mirror(x, 0)
        for bit in range((count - 1).bit_length()):
            rotate = functools.partial(lambda y, step: mirror(mirror(y, 0), step), step=2**bit)
            x = lax.cond((turn >> bit) & 1 == 1, rotate, lambda y: y, x)
        return x

    recv_x = lax.cond((shift <= 1) | (shift >= C - 3), third_block, lambda x: x, send_x)

    recv_a = lax.ppermute(send_a, "ja", rows_a)
    recv_b = lax.ppermute(send_b, "ja", rows_b)
    send_e, send_o = pl.pallas_call(
        ghost_kernel,
        in_specs=[vmem] * 4,
        out_specs=[vmem] * 2,
        out_shape=[planes(3), planes(3)],
        name="pack_ghost_columns",
    )(columns_e, columns_o, recv_a, recv_b)
    recv_e = lax.ppermute(send_e, "ia", even)
    recv_o = lax.ppermute(send_o, "ia", odd)

    def fold_and_inner(q, send_b, raw):
        near = lax.ppermute(send_b, both, fold(q))
        far = lax.ppermute(send_b, both, fold((q - 1) % count))
        inner = pl.pallas_call(
            inner_kernel,
            in_specs=[hbm] * 4,
            out_specs=vmem,
            out_shape=planes(R - 6),
            scratch_shapes=RAW_SCRATCH,
            compiler_params=big,
            cost_estimate=cost(2 * 10**8, 16 * 10**6),
            name="inner",
        )(*raw)
        return near, far, inner

    near, far, inner = lax.switch(
        block, [functools.partial(fold_and_inner, q) for q in range(count)], send_b, raw
    )
    return pl.pallas_call(
        finish_kernel,
        in_specs=[pl.BlockSpec(memory_space=pltpu.SMEM)] + [hbm] * 5 + [vmem] + [hbm] * 7 + [vmem],
        out_specs=hbm,
        out_shape=jax.ShapeDtypeStruct((V, L, R, C), jnp.float32),
        scratch_shapes=[
            scratch(8), scratch(8), scratch(), scratch(3), scratch(3), scratch(8),
            scratch(3, PLANES), scratch(2, PLANES), scratch(R), scratch(R),
            pltpu.VMEM((V, SLOTS, C), jnp.float32), pltpu.VMEM((V, SLOTS, 2 * C), jnp.bfloat16),
        ] + RAW_SCRATCH + [pltpu.SemaphoreType.DMA((7,)), pltpu.SemaphoreType.DMA((V,))],
        compiler_params=big,
        name="finish",
    )(
        partner, *raw, inner, jnp.swapaxes(vertical, 0, 1), strips,
        recv_a, recv_b, near, far, recv_e, recv_o, recv_x,
    )


def solution(mesh):
    placed = (
        P(None, None, "ja", "ia"),
        P(None, None, "ja", "ia"),
        P(None, None, "ja", "ia"),
        P(None, "ja", "ia"),
        P(),
        P(),
    )
    return jax.shard_map(
        body, mesh=mesh, in_specs=placed, out_specs=P(None, None, "ja", "ia"), check_vma=False
    )
```

```python
import functools
import numpy as np
import jax
import jax.numpy as jnp
from jax import lax
from jax.experimental import pallas as pl
from jax.experimental.pallas import tpu as pltpu
from jax.sharding import PartitionSpec as P

ITERS = 4
diff_ceiling = 8.0
V, L, R, C = 2, 75, 32, 128
SLOTS = 80
DEPTH = V * SLOTS
CENTRE, HALF = 33.0, 32.0
ROOT_SCALE = 32.0**-0.5


def chebyshev_steps(count):
    lowest_eig = 1.0
    highest_eig = 1.0 + 8.0 * diff_ceiling
    centre_val = 0.5 * (highest_eig + lowest_eig)
    half_width = 0.5 * (highest_eig - lowest_eig)
    plan = []
    step_size = 1.0 / centre_val
    momentum = 0.0
    plan.append((step_size, momentum))
    for turn_index in range(1, count):
        if turn_index == 1:
            momentum = 0.5 * (half_width * step_size) ** 2
        else:
            momentum = (0.5 * half_width * step_size) ** 2
        step_size = 1.0 / (centre_val - momentum / step_size)
        plan.append((step_size, momentum))
    return plan


def polynomial():
    poly = np.polynomial.polynomial
    operator = np.array([CENTRE, HALF])
    iterate = np.zeros(1)
    residual = np.ones(1)
    direction = np.zeros(1)
    for turn_index, (step_size, momentum) in enumerate(chebyshev_steps(ITERS)):
        direction = poly.polyadd(residual, momentum * direction)
        iterate = poly.polyadd(iterate, step_size * direction)
        if turn_index < ITERS - 1:
            residual = poly.polysub(residual, step_size * poly.polymul(operator, direction))
    return [float(c) for c in iterate]


POLY = polynomial()
LEAD = POLY[3]
B2, B1, B0 = POLY[2] / LEAD, POLY[1] / LEAD, POLY[0] / LEAD

GHOST = [(0, 1), (0, 2), (0, 3), (1, 1), (1, 2), (2, 1), (2, 2), (2, 3)]
PLANES = 5


def place(r):
    return divmod(r + 3, PLANES)


def lanes(rows):
    return lax.broadcasted_iota(jnp.int32, (rows, C), 1)


def roll(x, by):
    if isinstance(by, int):
        by = by % C
        return pltpu.roll(x, by, 1) if by else x
    return pltpu.roll(x, by & (C - 1), 1)


def slot_of(lane):
    return ((lane + 8) >> 4) & 7


def parities():
    return (lax.axis_index("ia") & 1) == 1, (lax.axis_index("ja") & 1) == 1


PARTS = [(0, 0, L), (1, 0, L)]
LAND_PARTS = [(0, L)]


def start_rows(raw, kept, sems, spans):
    land, ls = raw[3], kept[3]
    for c, (v, level, depth) in enumerate(PARTS):
        source = pl.ds(level, depth)
        at = pl.ds(v * SLOTS + level, depth)
        for low, count in spans:

            def row(r, carry):
                for j in range(3):
                    pltpu.make_async_copy(raw[j].at[v, source, r], kept[j].at[r, at], sems.at[3 * c + j]).start()
                return carry

            lax.fori_loop(low, low + count, row, 0)


def start_land(land, ls, sems, spans):
    for c, (level, depth) in enumerate(LAND_PARTS):
        at = pl.ds(level, depth)
        for low, count in spans:

            def row(r, carry):
                pltpu.make_async_copy(land.at[at, r], ls.at[r, at], sems.at[9 + c]).start()
                return carry

            lax.fori_loop(low, low + count, row, 0)


def wait_for(ref, sem):
    pltpu.make_async_copy(ref, ref, sem).wait()


def wait_rows(kept, sems, c, count):
    v, level, depth = PARTS[c]
    for j in range(3):
        wait_for(kept[j].at[pl.ds(0, count), pl.ds(v * SLOTS + level, depth)], sems.at[3 * c + j])


def wait_land(ls, sems, c, count):
    level, depth = LAND_PARTS[c]
    wait_for(ls.at[pl.ds(0, count), pl.ds(level, depth)], sems.at[9 + c])


def root(x):
    return x * lax.rsqrt(x)


def span(tall, t):
    return pl.ds(pl.multiple_of(tall * t, 8), tall)


def cell(kept, tall, t, r):
    f, di, dj, ls = kept
    at = span(tall, t)
    wet = ls[r, span(tall, lax.rem(t, SLOTS // tall)), :].astype(jnp.float32)
    scaled = wet * ROOT_SCALE
    return f[r, at, :] * wet, root(di[r, at, :]) * scaled, root(dj[r, at, :]) * scaled


RAW_SCRATCH = [
    pltpu.VMEM((R, DEPTH, C), jnp.float32),
    pltpu.VMEM((R, DEPTH, C), jnp.float32),
    pltpu.VMEM((R, DEPTH, C), jnp.float32),
    pltpu.VMEM((R, SLOTS, C), jnp.int32),
    pltpu.SemaphoreType.DMA((11,)),
]
ALL_ROWS = [(0, R)]


def tiles(kept, sems, count, tall, tile, land_rows=0):
    def body(t, carry):
        for c, (v, level, depth) in enumerate(PARTS):

            @pl.when(t == (v * SLOTS + level) // tall)
            def _():
                if land_rows and c < len(LAND_PARTS):
                    wait_land(kept[3], sems, c, land_rows)
                wait_rows(kept, sems, c, count)

        tile(t)
        return carry

    lax.fori_loop(0, DEPTH // tall, body, 0)


EDGE = 6
EDGE_ROWS = [(0, EDGE), (R - EDGE, EDGE)]
OUTER_ROWS = [(0, 3), (R - 3, 3)]


ROWS_TALL = 40
COLUMNS_TALL = 40


def rows_kernel(
    field, diff_i, diff_j, land, partner, send_a, send_b, send_x, block, special, centre, centre_sem,
    f, di, dj, ls, sems,
):
    centre_copy = pltpu.make_async_copy(partner.at[pl.ds(0, C)], centre, centre_sem)
    centre_copy.start()
    _, j_odd = parities()
    kept = (f, di, dj, ls)
    start_land(land, ls, sems, OUTER_ROWS)
    start_rows((field, diff_i, diff_j, land), kept, sems, OUTER_ROWS)
    slot = slot_of(lanes(ROWS_TALL))

    def tile(t):
        rows = span(ROWS_TALL, t)
        edge = {r: cell(kept, ROWS_TALL, t, r) for r in (0, 1, 2, R - 3, R - 2, R - 1)}
        third = jnp.zeros((ROWS_TALL, C), jnp.float32)
        for g, (a, far) in enumerate(GHOST):
            top, bottom = edge[R - far][a], edge[far - 1][a]
            send_a[g, rows, :] = jnp.where(j_odd, bottom, top)
            send_b[g, rows, :] = jnp.where(j_odd, top, bottom)
            third = jnp.where(slot == g, roll(top, 16 * g), third)
        send_x[rows, :] = third

    tiles(kept, sems, 6, ROWS_TALL, tile, 6)
    centre_copy.wait()
    block[0] = centre[0] >> 7
    shift = centre[0] & (C - 1)
    special[0] = jnp.where((shift <= 1) | (shift >= C - 3), 1, 0)


def columns_kernel(
    field, diff_i, diff_j, land, columns_e, columns_o, strips, packed_rows, out_sem, f, di, dj, ls, sems
):
    i_odd, _ = parities()
    kept = (f, di, dj, ls)
    start_land(land, ls, sems, ALL_ROWS)
    start_rows((field, diff_i, diff_j, land), kept, sems, ALL_ROWS)
    lane = lanes(COLUMNS_TALL)
    slot = slot_of(lane)
    in_slot = lane & 15
    def tile(t):
        rows = span(COLUMNS_TALL, t)
        packed = [[jnp.zeros((COLUMNS_TALL, C), jnp.float32) for _ in range(PLANES)] for _ in range(3)]
        for r in range(R):
            values = cell(kept, COLUMNS_TALL, t, r)
            index, p = place(r)
            for a in range(3):
                packed[a][p] = jnp.where(slot == index, roll(values[a], 16 * index), packed[a][p])
        for a in range(3):
            left, right = packed[a][0], packed[a][0]
            for p in range(PLANES):
                packed_rows[a, p, rows, :] = packed[a][p]
                if p:
                    left = jnp.where(in_slot >= 3 * p, roll(packed[a][p], 3 * p), left)
                    right = jnp.where(in_slot < 16 - 3 * p, roll(packed[a][p], -3 * p), right)
            columns_e[a, rows, :] = jnp.where(i_odd, left, right)
            columns_o[a, rows, :] = jnp.where(i_odd, right, left)
        pltpu.make_async_copy(packed_rows.at[:, :, rows], strips.at[:, :, rows], out_sem).start()

    tiles(kept, sems, R, COLUMNS_TALL, tile, R)
    wait_for(packed_rows, out_sem)


WIDE = 80


def ghost_kernel(columns_e, columns_o, recv_a, recv_b, send_e, send_o):
    i_odd, j_odd = parities()
    lane = lanes(WIDE)

    def tile(t, carry):
        rows = pl.ds(pl.multiple_of(WIDE * t, 8), WIDE)
        for a in range(3):
            got_e, got_o = columns_e[a, rows, :], columns_o[a, rows, :]
            left = jnp.where(i_odd, got_e, got_o)
            right = jnp.where(i_odd, got_o, got_e)
            for g, (b, far) in enumerate(GHOST):
                if a != b:
                    continue
                one, two = recv_a[g, rows, :], recv_b[g, rows, :]
                for r, ghost in ((-far, jnp.where(j_odd, one, two)), (R - 1 + far, jnp.where(j_odd, two, one))):
                    at, p = place(r)
                    by = (16 * at + 3 * p) % C
                    here = (lane >= by) & (lane < by + 3)
                    left = jnp.where(here, roll(ghost, by), left)
                    by = (16 * at - 3 - 3 * p) % C
                    here = (lane >= by) & (lane < by + 3)
                    right = jnp.where(here, roll(ghost, by + 3), right)
            send_e[a, rows, :] = jnp.where(i_odd, left, right)
            send_o[a, rows, :] = jnp.where(i_odd, right, left)
        return carry

    lax.fori_loop(0, DEPTH // WIDE, tile, 0)


def zonal(u, edge):
    flux = edge * (u - roll(u, -1))
    return flux - roll(flux, 1)


def stream(low_row, high_row, data, emit, not_last):
    src, root_j, edge, vert, one, two = {}, {}, {}, {}, {}, {}
    n1, n2, n3 = {}, {}, {}
    lo, hi = low_row - 3, high_row + 2
    for r in range(lo, hi + 1):
        src[r], z, root_j[r] = data(r)
        if z is not None:
            edge[r] = z * not_last * roll(z, -1)
        if r == lo:
            continue
        p = r - 1
        vert[p] = root_j[p] * root_j[r]
        n1[p] = vert[p] * (src[p] - src[r])
        if p == lo:
            continue
        one[p] = (B2 - 1.0) * src[p] + zonal(src[p], edge[p]) + n1[p] - n1[p - 1]
        if p == lo + 1:
            continue
        q = p - 1
        n2[q] = vert[q] * (one[q] - one[p])
        if q == lo + 1:
            continue
        two[q] = B1 * src[q] - one[q] + zonal(one[q], edge[q]) + n2[q] - n2[q - 1]
        if q == lo + 2:
            continue
        t = q - 1
        n3[t] = vert[t] * (two[t] - two[q])
        if t == lo + 2:
            continue
        emit(t, B0 * src[t] - two[t] + zonal(two[t], edge[t]) + n3[t] - n3[t - 1])


def strip_rows(src, z, m):
    after = lambda x: [x[p + 1] if p + 1 < PLANES else roll(x[0], -16) for p in range(PLANES)]
    before = lambda x: [x[p - 1] if p else roll(x[PLANES - 1], 16) for p in range(PLANES)]
    edge = [x * roll(x, -1) for x in z]
    vert = [x * y for x, y in zip(m, after(m))]

    def apply(u, base):
        flux = [c * (x - y) for c, x, y in zip(vert, u, after(u))]
        return [
            b + zonal(x, e) + f - g
            for b, x, e, f, g in zip(base, u, edge, flux, before(flux))
        ]

    one = apply(src, [(B2 - 1.0) * s for s in src])
    two = apply(one, [B1 * s - u for s, u in zip(src, one)])
    return apply(two, [B0 * s - u for s, u in zip(src, two)])


INNER_TALL = 8


def inner_kernel(field, diff_i, diff_j, land, out, done, out_sem, f, di, dj, ls, sems):
    kept = (f, di, dj, ls)
    start_land(land, ls, sems, ALL_ROWS)
    start_rows((field, diff_i, diff_j, land), kept, sems, ALL_ROWS)
    not_last = jnp.where(lanes(INNER_TALL) == C - 1, 0.0, 1.0)

    def tile(t):
        rows = span(INNER_TALL, t)

        def emit(r, value):
            done[r - 3, rows, :] = value

        stream(3, R - 3, lambda r: cell(kept, INNER_TALL, t, r), emit, not_last)
        pltpu.make_async_copy(done.at[:, rows], out.at[:, rows], out_sem).start()

    tiles(kept, sems, R, INNER_TALL, tile, R)
    wait_for(done, out_sem)


STRIP_TALL = 160
EDGE_TALL = 80


def finish_kernel(
    field, diff_i, diff_j, land, inner, vertical, partner, strips,
    recv_a, recv_b, near, far, recv_e, recv_o, recv_x,
    out, north, south, north_halo, east, west, fold, own_strips, fixed, diffused, mixed, square, weights, centre, centre_sem,
    f, di, dj, ls, sems, got, out_sem,
):
    i_odd, j_odd = parities()
    at_top = lax.axis_index("ja") == 3
    at_bottom = lax.axis_index("ja") == 0
    centre_copy = pltpu.make_async_copy(partner.at[pl.ds(0, C)], centre, centre_sem)
    centre_copy.start()
    kept = (f, di, dj, ls)

    def choose(flag, first, second, to, sem):
        @pl.when(flag)
        def _():
            pltpu.make_async_copy(first, to, sem).start()

        @pl.when(jnp.logical_not(flag))
        def _():
            pltpu.make_async_copy(second, to, sem).start()

    choose(i_odd, recv_o, recv_e, east, got.at[0])
    choose(i_odd, recv_e, recv_o, west, got.at[1])
    choose(j_odd, recv_a, recv_b, south, got.at[3])

    @pl.when(at_top)
    def _():
        pltpu.make_async_copy(near, north, got.at[2]).start()
        pltpu.make_async_copy(far, fold, got.at[4]).start()

    @pl.when(jnp.logical_not(at_top))
    def _():
        choose(j_odd, recv_b, recv_a, north, got.at[2])

    strips_copy = pltpu.make_async_copy(strips, own_strips, got.at[6])
    strips_copy.start()
    start_rows((field, diff_i, diff_j, land), kept, sems, EDGE_ROWS)
    start_land(land, ls, sems, ALL_ROWS)
    inner_copy = pltpu.make_async_copy(inner, diffused.at[pl.ds(3, R - 6)], got.at[5])
    inner_copy.start()

    square[...] = jnp.zeros_like(square)
    for v in range(V):
        square[v, pl.ds(0, L), pl.ds(0, L)] = vertical[:, v, :] * np.float32(LEAD)
        high = square[v].astype(jnp.bfloat16).astype(jnp.float32)
        rest = square[v] - high
        pad = jnp.zeros_like(high)
        high = jnp.concatenate([high, pad], axis=1)
        rest = jnp.concatenate([rest, pad], axis=1)
        both = high + pltpu.roll(high, SLOTS, 1) + pltpu.roll(rest, 2 * SLOTS, 1)
        weights[v] = both.astype(jnp.bfloat16)

    for j, ref in enumerate((east, west, north, south)):
        wait_for(ref, got.at[j])

    centre_copy.wait()
    shift = centre[0] & (C - 1)

    @pl.when(at_top)
    def _():
        wait_for(fold, got.at[4])
        wide = lanes(DEPTH)
        wide_slot = slot_of(wide)
        index = (shift - wide) & (C - 1)
        inside = wide <= shift
        beyond = ((shift <= 1) & (wide >= C - 2)) | ((shift >= C - 3) & (wide <= 2))

        def ghost(g, carry):
            one, two, three = north[g], fold[g], roll(recv_x[...], -16 * g)
            own = jnp.where(inside, one, two)
            other = jnp.where(beyond, three, jnp.where(inside, two, one))
            north[g] = jnp.take_along_axis(own, index, axis=1)
            other = roll(jnp.take_along_axis(other, index, axis=1), 16 * g)
            north_halo[...] = jnp.where(wide_slot == g, other, north_halo[...])
            return carry

        lax.fori_loop(0, 8, ghost, 0)

    @pl.when(at_bottom)
    def _():
        south[...] = jnp.zeros_like(south)

    strips_copy.wait()
    lane = lanes(STRIP_TALL)
    in_slot = lane & 15
    slot = slot_of(lane)
    zero = jnp.zeros((STRIP_TALL, C), jnp.float32)

    def strip_tile(n, carry):
        t, side = n >> 1, n & 1
        rows = span(STRIP_TALL, t)
        outside = ((side == 0) & (in_slot >= 13)) | ((side == 1) & (in_slot < 3))
        packed = [[None] * PLANES for _ in range(3)]
        for a in range(3):
            got_east, got_west = east[a, rows, :], west[a, rows, :]
            for p in range(PLANES):
                own = own_strips[a, p, rows, :]
                halo = jnp.where(in_slot < 8, roll(got_east, -3 * p), roll(got_west, 3 * p))
                for r in (-3, -2, -1, R, R + 1, R + 2):
                    at, plane = place(r)
                    if plane != p:
                        continue
                    far_off = -r if r < 0 else r - R + 1
                    mine, theirs = zero, zero
                    if (a, far_off) in GHOST:
                        g = GHOST.index((a, far_off))
                        mine = roll((south if r < 0 else north)[g, rows, :], 16 * at)
                        theirs = roll(north_halo[rows, :], 16 * (at - g))
                    here = slot == at
                    own = jnp.where(here, mine, own)
                    if r >= R:
                        halo = jnp.where(here & at_top, theirs, halo)
                packed[a][p] = jnp.where(outside, halo, own)
        for p, value in enumerate(strip_rows(*packed)):
            fixed[side, p, rows, :] = value
        return carry

    lax.fori_loop(0, 2 * (DEPTH // STRIP_TALL), strip_tile, 0)

    not_last = jnp.where(lanes(EDGE_TALL) == C - 1, 0.0, 1.0)
    for c in range(len(LAND_PARTS)):
        wait_land(ls, sems, c, R)

    def edge_tile(t, low):
        rows = span(EDGE_TALL, t)

        def ghost(r):
            planes, far_off = (south, -r) if r < 0 else (north, r - R + 1)
            pick = lambda g: planes[g, rows, :]
            return (pick(far_off - 1), pick(far_off + 2) if far_off <= 2 else None, pick(far_off + 4))

        def emit(r, value):
            diffused[r, rows, :] = value

        data = lambda r: cell(kept, EDGE_TALL, t, r) if 0 <= r < R else ghost(r)
        stream(low, low + 3, data, emit, not_last)

    tiles(kept, sems, 2 * EDGE, EDGE_TALL, lambda t: edge_tile(t, 0))

    def upper(t, carry):
        edge_tile(t, R - 3)
        return carry

    lax.fori_loop(0, DEPTH // EDGE_TALL, upper, 0)
    inner_copy.wait()

    wide = lanes(SLOTS)
    from_left = (wide & 15) < 8
    seam = (wide < 3) | (wide >= C - 3)
    real = lax.broadcasted_iota(jnp.int32, (SLOTS, C), 0) < L
    tail = jnp.zeros((2 * C - 3 * SLOTS, 2 * C), jnp.bfloat16)

    for v in range(V):
        at = pl.ds(v * SLOTS, SLOTS)

        def pair_of_rows(pair, carry):
            halves = []
            for side in range(2):
                r = 2 * pair + side
                place_of = lax.div(r + 3, PLANES)
                p = r + 3 - PLANES * place_of
                columns = roll(jnp.where(from_left, fixed[0, p, at], fixed[1, p, at]), -16 * place_of)
                halves.append(jnp.where(real, jnp.where(seam, columns, diffused[r, at]), 0.0))
            values = jnp.concatenate(halves, axis=1)
            high = values.astype(jnp.bfloat16)
            rest = (values - high.astype(jnp.float32)).astype(jnp.bfloat16)
            stacked = jnp.concatenate([high, rest, high, tail], axis=0)
            result = jnp.dot(weights[v], stacked, preferred_element_type=jnp.float32)
            for side in range(2):
                r = 2 * pair + side
                mixed[r, at] = result[:, side * C : (side + 1) * C] * ls[r].astype(jnp.float32)
                pltpu.make_async_copy(mixed.at[r, pl.ds(v * SLOTS, L)], out.at[v, :, r], out_sem.at[v]).start()
            return carry

        lax.fori_loop(0, R // 2, pair_of_rows, 0, unroll=2)

    for v in range(V):
        wait_for(mixed.at[:, pl.ds(v * SLOTS, L)], out_sem.at[v])


def odd_partner(i, count):
    return (((i - 1) % count) ^ 1) + 1


def body(field, diff_i, diff_j, land_sea, partner, vertical):
    count = lax.axis_size("ia")
    raw = (field, diff_i, diff_j, land_sea)
    hbm = pl.BlockSpec(memory_space=pltpu.HBM)
    vmem = pl.BlockSpec(memory_space=pltpu.VMEM)
    planes = lambda *n: jax.ShapeDtypeStruct(n + (DEPTH, C), jnp.float32)
    scratch = lambda *n: pltpu.VMEM(n + (DEPTH, C), jnp.float32)
    big = pltpu.CompilerParams(vmem_limit_bytes=60 * 2**20)

    def cost(flops, size):
        return pl.CostEstimate(flops=flops, bytes_accessed=size, transcendentals=0)

    smem = pl.BlockSpec(memory_space=pltpu.SMEM)
    number = jax.ShapeDtypeStruct((1,), jnp.int32)
    send_a, send_b, send_x, block, special = pl.pallas_call(
        rows_kernel,
        in_specs=[hbm] * 5,
        out_specs=[vmem] * 3 + [smem] * 2,
        out_shape=[planes(8), planes(8), planes(), number, number],
        scratch_shapes=[pltpu.SMEM((C,), jnp.int32), pltpu.SemaphoreType.DMA] + RAW_SCRATCH,
        compiler_params=big,
        name="pack_rows",
    )(*raw, partner)
    block, special = block.reshape(()), special.reshape(())
    columns_e, columns_o, strips = pl.pallas_call(
        columns_kernel,
        in_specs=[hbm] * 4,
        out_specs=[vmem] * 2 + [hbm],
        out_shape=[planes(3), planes(3), planes(3, PLANES)],
        scratch_shapes=[scratch(3, PLANES), pltpu.SemaphoreType.DMA] + RAW_SCRATCH,
        compiler_params=big,
        cost_estimate=cost(10**8, 16 * 10**6),
        name="pack_columns",
    )(*raw)

    both = ("ia", "ja")
    rows_a = [(0, 1), (1, 0), (2, 3), (3, 2)]
    rows_b = [(1, 2), (2, 1)]
    even = [(i, i ^ 1) for i in range(count)]
    odd = [(i, odd_partner(i, count) % count) for i in range(count)]

    def fold(q):
        return [(t * 4 + 3, ((q - t) % count) * 4 + 3) for t in range(count)]

    def mirror(x, q):
        return lax.ppermute(x, both, fold(q))

    def third_block(x):
        turn = jnp.where(partner[0] & (C - 1) <= 1, block - 2, block + 1)
        x = mirror(x, 0)
        for bit in range((count - 1).bit_length()):
            rotate = functools.partial(lambda y, step: mirror(mirror(y, 0), step), step=2**bit)
            x = lax.cond((turn >> bit) & 1 == 1, rotate, lambda y: y, x)
        return x

    recv_x = lax.cond(special == 1, third_block, lambda x: x, send_x)

    recv_a = lax.ppermute(send_a, "ja", rows_a)
    recv_b = lax.ppermute(send_b, "ja", rows_b)
    send_e, send_o = pl.pallas_call(
        ghost_kernel,
        in_specs=[vmem] * 4,
        out_specs=[vmem] * 2,
        out_shape=[planes(3), planes(3)],
        name="pack_ghost_columns",
    )(columns_e, columns_o, recv_a, recv_b)
    recv_e = lax.ppermute(send_e, "ia", even)
    recv_o = lax.ppermute(send_o, "ia", odd)

    def fold_and_inner(q, send_b, raw):
        near = lax.ppermute(send_b, both, fold(q))
        far = lax.ppermute(send_b, both, fold((q - 1) % count))
        inner = pl.pallas_call(
            inner_kernel,
            in_specs=[hbm] * 4,
            out_specs=hbm,
            out_shape=planes(R - 6),
            scratch_shapes=[scratch(R - 6), pltpu.SemaphoreType.DMA] + RAW_SCRATCH,
            compiler_params=big,
            cost_estimate=cost(2 * 10**8, 16 * 10**6),
            name="inner",
        )(*raw)
        return near, far, inner

    near, far, inner = lax.switch(
        block, [functools.partial(fold_and_inner, q) for q in range(count)], send_b, raw
    )
    return pl.pallas_call(
        finish_kernel,
        in_specs=[hbm] * 5 + [vmem] + [hbm] * 8 + [vmem],
        out_specs=hbm,
        out_shape=jax.ShapeDtypeStruct((V, L, R, C), jnp.float32),
        scratch_shapes=[
            scratch(8), scratch(8), scratch(), scratch(3), scratch(3), scratch(8),
            scratch(3, PLANES), scratch(2, PLANES), scratch(R), scratch(R),
            pltpu.VMEM((V, SLOTS, C), jnp.float32), pltpu.VMEM((V, SLOTS, 2 * C), jnp.bfloat16),
            pltpu.SMEM((C,), jnp.int32), pltpu.SemaphoreType.DMA,
        ] + RAW_SCRATCH + [pltpu.SemaphoreType.DMA((7,)), pltpu.SemaphoreType.DMA((V,))],
        compiler_params=big,
        name="finish",
    )(
        *raw, inner, jnp.swapaxes(vertical, 0, 1), partner, strips,
        recv_a, recv_b, near, far, recv_e, recv_o, recv_x,
    )


def solution(mesh):
    placed = (
        P(None, None, "ja", "ia"),
        P(None, None, "ja", "ia"),
        P(None, None, "ja", "ia"),
        P(None, "ja", "ia"),
        P(),
        P(),
    )
    return jax.shard_map(
        body, mesh=mesh, in_specs=placed, out_specs=P(None, None, "ja", "ia"), check_vma=False
    )
```

```python
import functools
import numpy as np
import jax
import jax.numpy as jnp
from jax import lax
from jax.experimental import pallas as pl
from jax.experimental.pallas import tpu as pltpu
from jax.sharding import PartitionSpec as P

ITERS = 4
diff_ceiling = 8.0
V, L, R, C = 2, 75, 32, 128
SLOTS = 80
DEPTH = V * SLOTS
CENTRE, HALF = 33.0, 32.0
ROOT_SCALE = 32.0**-0.5


def chebyshev_steps(count):
    lowest_eig = 1.0
    highest_eig = 1.0 + 8.0 * diff_ceiling
    centre_val = 0.5 * (highest_eig + lowest_eig)
    half_width = 0.5 * (highest_eig - lowest_eig)
    plan = []
    step_size = 1.0 / centre_val
    momentum = 0.0
    plan.append((step_size, momentum))
    for turn_index in range(1, count):
        if turn_index == 1:
            momentum = 0.5 * (half_width * step_size) ** 2
        else:
            momentum = (0.5 * half_width * step_size) ** 2
        step_size = 1.0 / (centre_val - momentum / step_size)
        plan.append((step_size, momentum))
    return plan


def polynomial():
    poly = np.polynomial.polynomial
    operator = np.array([CENTRE, HALF])
    iterate = np.zeros(1)
    residual = np.ones(1)
    direction = np.zeros(1)
    for turn_index, (step_size, momentum) in enumerate(chebyshev_steps(ITERS)):
        direction = poly.polyadd(residual, momentum * direction)
        iterate = poly.polyadd(iterate, step_size * direction)
        if turn_index < ITERS - 1:
            residual = poly.polysub(residual, step_size * poly.polymul(operator, direction))
    return [float(c) for c in iterate]


POLY = polynomial()
LEAD = POLY[3]
B2, B1, B0 = POLY[2] / LEAD, POLY[1] / LEAD, POLY[0] / LEAD

GHOST = [(0, 1), (0, 2), (0, 3), (1, 1), (1, 2), (2, 1), (2, 2), (2, 3)]
PLANES = 5


def place(r):
    return divmod(r + 3, PLANES)


def lanes(rows):
    return lax.broadcasted_iota(jnp.int32, (rows, C), 1)


def roll(x, by):
    if isinstance(by, int):
        by = by % C
        return pltpu.roll(x, by, 1) if by else x
    return pltpu.roll(x, by & (C - 1), 1)


def slot_of(lane):
    return ((lane + 8) >> 4) & 7


def parities():
    return (lax.axis_index("ia") & 1) == 1, (lax.axis_index("ja") & 1) == 1


PARTS = [(0, 0, L), (1, 0, L)]
LAND_PARTS = [(0, L)]


def start_rows(raw, kept, sems, spans):
    land, ls = raw[3], kept[3]
    for c, (v, level, depth) in enumerate(PARTS):
        source = pl.ds(level, depth)
        at = pl.ds(v * SLOTS + level, depth)
        for low, count in spans:

            def row(r, carry):
                for j in range(3):
                    pltpu.make_async_copy(raw[j].at[v, source, r], kept[j].at[r, at], sems.at[3 * c + j]).start()
                return carry

            lax.fori_loop(low, low + count, row, 0)


def start_land(land, ls, sems, spans):
    for c, (level, depth) in enumerate(LAND_PARTS):
        at = pl.ds(level, depth)
        for low, count in spans:

            def row(r, carry):
                pltpu.make_async_copy(land.at[at, r], ls.at[r, at], sems.at[9 + c]).start()
                return carry

            lax.fori_loop(low, low + count, row, 0)


def wait_for(ref, sem):
    pltpu.make_async_copy(ref, ref, sem).wait()


def wait_rows(kept, sems, c, count):
    v, level, depth = PARTS[c]
    for j in range(3):
        wait_for(kept[j].at[pl.ds(0, count), pl.ds(v * SLOTS + level, depth)], sems.at[3 * c + j])


def wait_land(ls, sems, c, count):
    level, depth = LAND_PARTS[c]
    wait_for(ls.at[pl.ds(0, count), pl.ds(level, depth)], sems.at[9 + c])


def root(x):
    return x * lax.rsqrt(x)


def span(tall, t):
    return pl.ds(pl.multiple_of(tall * t, 8), tall)


def cell(kept, tall, t, r):
    f, di, dj, ls = kept
    at = span(tall, t)
    wet = ls[r, span(tall, lax.rem(t, SLOTS // tall)), :].astype(jnp.float32)
    scaled = wet * ROOT_SCALE
    return f[r, at, :] * wet, root(di[r, at, :]) * scaled, root(dj[r, at, :]) * scaled


RAW_SCRATCH = [
    pltpu.VMEM((R, DEPTH, C), jnp.float32),
    pltpu.VMEM((R, DEPTH, C), jnp.float32),
    pltpu.VMEM((R, DEPTH, C), jnp.float32),
    pltpu.VMEM((R, SLOTS, C), jnp.int32),
    pltpu.SemaphoreType.DMA((11,)),
]
ALL_ROWS = [(0, R)]


def tiles(kept, sems, count, tall, tile, land_rows=0):
    def body(t, carry):
        for c, (v, level, depth) in enumerate(PARTS):

            @pl.when(t == (v * SLOTS + level) // tall)
            def _():
                if land_rows and c < len(LAND_PARTS):
                    wait_land(kept[3], sems, c, land_rows)
                wait_rows(kept, sems, c, count)

        tile(t)
        return carry

    lax.fori_loop(0, DEPTH // tall, body, 0)


EDGE = 6
EDGE_ROWS = [(0, EDGE), (R - EDGE, EDGE)]
OUTER_ROWS = [(0, 3), (R - 3, 3)]


ROWS_TALL = 40
COLUMNS_TALL = 40


def rows_kernel(
    field, diff_i, diff_j, land, partner, send_a, send_b, send_x, block, special, centre, centre_sem,
    f, di, dj, ls, sems,
):
    centre_copy = pltpu.make_async_copy(partner.at[pl.ds(0, C)], centre, centre_sem)
    centre_copy.start()
    _, j_odd = parities()
    kept = (f, di, dj, ls)
    start_land(land, ls, sems, OUTER_ROWS)
    start_rows((field, diff_i, diff_j, land), kept, sems, OUTER_ROWS)
    slot = slot_of(lanes(ROWS_TALL))

    def tile(t):
        rows = span(ROWS_TALL, t)
        edge = {r: cell(kept, ROWS_TALL, t, r) for r in (0, 1, 2, R - 3, R - 2, R - 1)}
        third = jnp.zeros((ROWS_TALL, C), jnp.float32)
        for g, (a, far) in enumerate(GHOST):
            top, bottom = edge[R - far][a], edge[far - 1][a]
            send_a[g, rows, :] = jnp.where(j_odd, bottom, top)
            send_b[g, rows, :] = jnp.where(j_odd, top, bottom)
            third = jnp.where(slot == g, roll(top, 16 * g), third)
        send_x[rows, :] = third

    tiles(kept, sems, 6, ROWS_TALL, tile, 6)
    centre_copy.wait()
    block[0] = centre[0] >> 7
    shift = centre[0] & (C - 1)
    special[0] = jnp.where((shift <= 1) | (shift >= C - 3), 1, 0)


def columns_kernel(
    field, diff_i, diff_j, land, columns_e, columns_o, strips, packed_rows, out_sem, f, di, dj, ls, sems
):
    i_odd, _ = parities()
    kept = (f, di, dj, ls)
    start_land(land, ls, sems, ALL_ROWS)
    start_rows((field, diff_i, diff_j, land), kept, sems, ALL_ROWS)
    lane = lanes(COLUMNS_TALL)
    slot = slot_of(lane)
    in_slot = lane & 15
    def tile(t):
        rows = span(COLUMNS_TALL, t)
        packed = [[jnp.zeros((COLUMNS_TALL, C), jnp.float32) for _ in range(PLANES)] for _ in range(3)]
        for r in range(R):
            values = cell(kept, COLUMNS_TALL, t, r)
            index, p = place(r)
            for a in range(3):
                packed[a][p] = jnp.where(slot == index, roll(values[a], 16 * index), packed[a][p])
        for a in range(3):
            left, right = packed[a][0], packed[a][0]
            for p in range(PLANES):
                packed_rows[a, p, rows, :] = packed[a][p]
                if p:
                    left = jnp.where(in_slot >= 3 * p, roll(packed[a][p], 3 * p), left)
                    right = jnp.where(in_slot < 16 - 3 * p, roll(packed[a][p], -3 * p), right)
            columns_e[a, rows, :] = jnp.where(i_odd, left, right)
            columns_o[a, rows, :] = jnp.where(i_odd, right, left)
        pltpu.make_async_copy(packed_rows.at[:, :, rows], strips.at[:, :, rows], out_sem).start()

    tiles(kept, sems, R, COLUMNS_TALL, tile, R)
    wait_for(packed_rows, out_sem)


WIDE = 80


def ghost_kernel(columns_e, columns_o, recv_a, recv_b, send_e, send_o):
    i_odd, j_odd = parities()
    lane = lanes(WIDE)

    def tile(t, carry):
        rows = pl.ds(pl.multiple_of(WIDE * t, 8), WIDE)
        for a in range(3):
            got_e, got_o = columns_e[a, rows, :], columns_o[a, rows, :]
            left = jnp.where(i_odd, got_e, got_o)
            right = jnp.where(i_odd, got_o, got_e)
            for g, (b, far) in enumerate(GHOST):
                if a != b:
                    continue
                one, two = recv_a[g, rows, :], recv_b[g, rows, :]
                for r, ghost in ((-far, jnp.where(j_odd, one, two)), (R - 1 + far, jnp.where(j_odd, two, one))):
                    at, p = place(r)
                    by = (16 * at + 3 * p) % C
                    here = (lane >= by) & (lane < by + 3)
                    left = jnp.where(here, roll(ghost, by), left)
                    by = (16 * at - 3 - 3 * p) % C
                    here = (lane >= by) & (lane < by + 3)
                    right = jnp.where(here, roll(ghost, by + 3), right)
            send_e[a, rows, :] = jnp.where(i_odd, left, right)
            send_o[a, rows, :] = jnp.where(i_odd, right, left)
        return carry

    lax.fori_loop(0, DEPTH // WIDE, tile, 0)


def zonal(u, edge):
    flux = edge * (u - roll(u, -1))
    return flux - roll(flux, 1)


def stream(low_row, high_row, data, emit, not_last):
    src, root_j, edge, vert, one, two = {}, {}, {}, {}, {}, {}
    n1, n2, n3 = {}, {}, {}
    lo, hi = low_row - 3, high_row + 2
    for r in range(lo, hi + 1):
        src[r], z, root_j[r] = data(r)
        if z is not None:
            edge[r] = z * not_last * roll(z, -1)
        if r == lo:
            continue
        p = r - 1
        vert[p] = root_j[p] * root_j[r]
        n1[p] = vert[p] * (src[p] - src[r])
        if p == lo:
            continue
        one[p] = (B2 - 1.0) * src[p] + zonal(src[p], edge[p]) + n1[p] - n1[p - 1]
        if p == lo + 1:
            continue
        q = p - 1
        n2[q] = vert[q] * (one[q] - one[p])
        if q == lo + 1:
            continue
        two[q] = B1 * src[q] - one[q] + zonal(one[q], edge[q]) + n2[q] - n2[q - 1]
        if q == lo + 2:
            continue
        t = q - 1
        n3[t] = vert[t] * (two[t] - two[q])
        if t == lo + 2:
            continue
        emit(t, B0 * src[t] - two[t] + zonal(two[t], edge[t]) + n3[t] - n3[t - 1])


def strip_rows(src, z, m):
    after = lambda x: [x[p + 1] if p + 1 < PLANES else roll(x[0], -16) for p in range(PLANES)]
    before = lambda x: [x[p - 1] if p else roll(x[PLANES - 1], 16) for p in range(PLANES)]
    edge = [x * roll(x, -1) for x in z]
    vert = [x * y for x, y in zip(m, after(m))]

    def apply(u, base):
        flux = [c * (x - y) for c, x, y in zip(vert, u, after(u))]
        return [
            b + zonal(x, e) + f - g
            for b, x, e, f, g in zip(base, u, edge, flux, before(flux))
        ]

    one = apply(src, [(B2 - 1.0) * s for s in src])
    two = apply(one, [B1 * s - u for s, u in zip(src, one)])
    return apply(two, [B0 * s - u for s, u in zip(src, two)])


INNER_TALL = 8


def inner_kernel(field, diff_i, diff_j, land, out, done, out_sem, f, di, dj, ls, sems):
    kept = (f, di, dj, ls)
    start_land(land, ls, sems, ALL_ROWS)
    start_rows((field, diff_i, diff_j, land), kept, sems, ALL_ROWS)
    not_last = jnp.where(lanes(INNER_TALL) == C - 1, 0.0, 1.0)

    def tile(t):
        rows = span(INNER_TALL, t)

        def emit(r, value):
            done[r - 3, rows, :] = value

        stream(3, R - 3, lambda r: cell(kept, INNER_TALL, t, r), emit, not_last)
        pltpu.make_async_copy(done.at[:, rows], out.at[:, rows], out_sem).start()

    tiles(kept, sems, R, INNER_TALL, tile, R)
    wait_for(done, out_sem)


STRIP_TALL = 160
EDGE_TALL = 80


def finish_kernel(
    field, diff_i, diff_j, land, inner, vertical, partner, strips,
    recv_a, recv_b, near, far, recv_e, recv_o, recv_x,
    out, north, south, north_halo, east, west, fold, own_strips, fixed, diffused, mixed, square, weights, centre, centre_sem,
    f, di, dj, ls, sems, got, out_sem,
):
    i_odd, j_odd = parities()
    at_top = lax.axis_index("ja") == 3
    at_bottom = lax.axis_index("ja") == 0
    centre_copy = pltpu.make_async_copy(partner.at[pl.ds(0, C)], centre, centre_sem)
    centre_copy.start()
    kept = (f, di, dj, ls)

    def choose(flag, first, second, to, sem):
        @pl.when(flag)
        def _():
            pltpu.make_async_copy(first, to, sem).start()

        @pl.when(jnp.logical_not(flag))
        def _():
            pltpu.make_async_copy(second, to, sem).start()

    choose(i_odd, recv_o, recv_e, east, got.at[0])
    choose(i_odd, recv_e, recv_o, west, got.at[1])
    choose(j_odd, recv_a, recv_b, south, got.at[3])

    @pl.when(at_top)
    def _():
        pltpu.make_async_copy(near, north, got.at[2]).start()
        pltpu.make_async_copy(far, fold, got.at[4]).start()

    @pl.when(jnp.logical_not(at_top))
    def _():
        choose(j_odd, recv_b, recv_a, north, got.at[2])

    strips_copy = pltpu.make_async_copy(strips, own_strips, got.at[6])
    strips_copy.start()
    start_rows((field, diff_i, diff_j, land), kept, sems, EDGE_ROWS)
    start_land(land, ls, sems, ALL_ROWS)
    inner_copy = pltpu.make_async_copy(inner, diffused.at[pl.ds(3, R - 6)], got.at[5])
    inner_copy.start()

    square[...] = jnp.zeros_like(square)
    for v in range(V):
        square[v, pl.ds(0, L), pl.ds(0, L)] = vertical[:, v, :] * np.float32(LEAD)
        high = square[v].astype(jnp.bfloat16).astype(jnp.float32)
        rest = square[v] - high
        pad = jnp.zeros_like(high)
        high = jnp.concatenate([high, pad], axis=1)
        rest = jnp.concatenate([rest, pad], axis=1)
        both = high + pltpu.roll(high, SLOTS, 1) + pltpu.roll(rest, 2 * SLOTS, 1)
        weights[v] = both.astype(jnp.bfloat16)

    for j, ref in enumerate((east, west, north, south)):
        wait_for(ref, got.at[j])

    centre_copy.wait()
    shift = centre[0] & (C - 1)

    @pl.when(at_top)
    def _():
        wait_for(fold, got.at[4])
        wide = lanes(DEPTH)
        wide_slot = slot_of(wide)
        index = (shift - wide) & (C - 1)
        inside = wide <= shift
        beyond = ((shift <= 1) & (wide >= C - 2)) | ((shift >= C - 3) & (wide <= 2))

        def ghost(g, carry):
            one, two, three = north[g], fold[g], roll(recv_x[...], -16 * g)
            own = jnp.where(inside, one, two)
            other = jnp.where(beyond, three, jnp.where(inside, two, one))
            north[g] = jnp.take_along_axis(own, index, axis=1)
            other = roll(jnp.take_along_axis(other, index, axis=1), 16 * g)
            north_halo[...] = jnp.where(wide_slot == g, other, north_halo[...])
            return carry

        lax.fori_loop(0, 8, ghost, 0, unroll=2)

    @pl.when(at_bottom)
    def _():
        south[...] = jnp.zeros_like(south)

    strips_copy.wait()
    lane = lanes(STRIP_TALL)
    in_slot = lane & 15
    slot = slot_of(lane)
    zero = jnp.zeros((STRIP_TALL, C), jnp.float32)

    def strip_tile(n, carry):
        t, side = n >> 1, n & 1
        rows = span(STRIP_TALL, t)
        outside = ((side == 0) & (in_slot >= 13)) | ((side == 1) & (in_slot < 3))
        packed = [[None] * PLANES for _ in range(3)]
        for a in range(3):
            got_east, got_west = east[a, rows, :], west[a, rows, :]
            for p in range(PLANES):
                own = own_strips[a, p, rows, :]
                halo = jnp.where(in_slot < 8, roll(got_east, -3 * p), roll(got_west, 3 * p))
                for r in (-3, -2, -1, R, R + 1, R + 2):
                    at, plane = place(r)
                    if plane != p:
                        continue
                    far_off = -r if r < 0 else r - R + 1
                    mine, theirs = zero, zero
                    if (a, far_off) in GHOST:
                        g = GHOST.index((a, far_off))
                        mine = roll((south if r < 0 else north)[g, rows, :], 16 * at)
                        theirs = roll(north_halo[rows, :], 16 * (at - g))
                    here = slot == at
                    own = jnp.where(here, mine, own)
                    if r >= R:
                        halo = jnp.where(here & at_top, theirs, halo)
                packed[a][p] = jnp.where(outside, halo, own)
        for p, value in enumerate(strip_rows(*packed)):
            fixed[side, p, rows, :] = value
        return carry

    lax.fori_loop(0, 2 * (DEPTH // STRIP_TALL), strip_tile, 0)

    not_last = jnp.where(lanes(EDGE_TALL) == C - 1, 0.0, 1.0)
    for c in range(len(LAND_PARTS)):
        wait_land(ls, sems, c, R)

    def edge_tile(t, low):
        rows = span(EDGE_TALL, t)

        def ghost(r):
            planes, far_off = (south, -r) if r < 0 else (north, r - R + 1)
            pick = lambda g: planes[g, rows, :]
            return (pick(far_off - 1), pick(far_off + 2) if far_off <= 2 else None, pick(far_off + 4))

        def emit(r, value):
            diffused[r, rows, :] = value

        data = lambda r: cell(kept, EDGE_TALL, t, r) if 0 <= r < R else ghost(r)
        stream(low, low + 3, data, emit, not_last)

    tiles(kept, sems, 2 * EDGE, EDGE_TALL, lambda t: edge_tile(t, 0))

    def upper(t, carry):
        edge_tile(t, R - 3)
        return carry

    lax.fori_loop(0, DEPTH // EDGE_TALL, upper, 0)
    inner_copy.wait()

    wide = lanes(SLOTS)
    from_left = (wide & 15) < 8
    seam = (wide < 3) | (wide >= C - 3)
    real = lax.broadcasted_iota(jnp.int32, (SLOTS, C), 0) < L
    tail = jnp.zeros((2 * C - 3 * SLOTS, 2 * C), jnp.bfloat16)

    for v in range(V):
        at = pl.ds(v * SLOTS, SLOTS)

        def pair_of_rows(pair, carry):
            halves = []
            for side in range(2):
                r = 2 * pair + side
                place_of = lax.div(r + 3, PLANES)
                p = r + 3 - PLANES * place_of
                columns = roll(jnp.where(from_left, fixed[0, p, at], fixed[1, p, at]), -16 * place_of)
                halves.append(jnp.where(real, jnp.where(seam, columns, diffused[r, at]), 0.0))
            values = jnp.concatenate(halves, axis=1)
            high = values.astype(jnp.bfloat16)
            rest = (values - high.astype(jnp.float32)).astype(jnp.bfloat16)
            stacked = jnp.concatenate([high, rest, high, tail], axis=0)
            result = jnp.dot(weights[v], stacked, preferred_element_type=jnp.float32)
            for side in range(2):
                r = 2 * pair + side
                mixed[r, at] = result[:, side * C : (side + 1) * C] * ls[r].astype(jnp.float32)
                pltpu.make_async_copy(mixed.at[r, pl.ds(v * SLOTS, L)], out.at[v, :, r], out_sem.at[v]).start()
            return carry

        lax.fori_loop(0, R // 2, pair_of_rows, 0, unroll=4)

    for v in range(V):
        wait_for(mixed.at[:, pl.ds(v * SLOTS, L)], out_sem.at[v])


def odd_partner(i, count):
    return (((i - 1) % count) ^ 1) + 1


def body(field, diff_i, diff_j, land_sea, partner, vertical):
    count = lax.axis_size("ia")
    raw = (field, diff_i, diff_j, land_sea)
    hbm = pl.BlockSpec(memory_space=pltpu.HBM)
    vmem = pl.BlockSpec(memory_space=pltpu.VMEM)
    planes = lambda *n: jax.ShapeDtypeStruct(n + (DEPTH, C), jnp.float32)
    scratch = lambda *n: pltpu.VMEM(n + (DEPTH, C), jnp.float32)
    big = pltpu.CompilerParams(vmem_limit_bytes=60 * 2**20)

    def cost(flops, size):
        return pl.CostEstimate(flops=flops, bytes_accessed=size, transcendentals=0)

    smem = pl.BlockSpec(memory_space=pltpu.SMEM)
    number = jax.ShapeDtypeStruct((1,), jnp.int32)
    send_a, send_b, send_x, block, special = pl.pallas_call(
        rows_kernel,
        in_specs=[hbm] * 5,
        out_specs=[vmem] * 3 + [smem] * 2,
        out_shape=[planes(8), planes(8), planes(), number, number],
        scratch_shapes=[pltpu.SMEM((C,), jnp.int32), pltpu.SemaphoreType.DMA] + RAW_SCRATCH,
        compiler_params=big,
        name="pack_rows",
    )(*raw, partner)
    block, special = block.reshape(()), special.reshape(())
    columns_e, columns_o, strips = pl.pallas_call(
        columns_kernel,
        in_specs=[hbm] * 4,
        out_specs=[vmem] * 2 + [hbm],
        out_shape=[planes(3), planes(3), planes(3, PLANES)],
        scratch_shapes=[scratch(3, PLANES), pltpu.SemaphoreType.DMA] + RAW_SCRATCH,
        compiler_params=big,
        cost_estimate=cost(10**8, 16 * 10**6),
        name="pack_columns",
    )(*raw)

    both = ("ia", "ja")
    rows_a = [(0, 1), (1, 0), (2, 3), (3, 2)]
    rows_b = [(1, 2), (2, 1)]
    even = [(i, i ^ 1) for i in range(count)]
    odd = [(i, odd_partner(i, count) % count) for i in range(count)]

    def fold(q):
        return [(t * 4 + 3, ((q - t) % count) * 4 + 3) for t in range(count)]

    def mirror(x, q):
        return lax.ppermute(x, both, fold(q))

    def third_block(x):
        turn = jnp.where(partner[0] & (C - 1) <= 1, block - 2, block + 1)
        x = mirror(x, 0)
        for bit in range((count - 1).bit_length()):
            rotate = functools.partial(lambda y, step: mirror(mirror(y, 0), step), step=2**bit)
            x = lax.cond((turn >> bit) & 1 == 1, rotate, lambda y: y, x)
        return x

    recv_x = lax.cond(special == 1, third_block, lambda x: x, send_x)

    recv_a = lax.ppermute(send_a, "ja", rows_a)
    recv_b = lax.ppermute(send_b, "ja", rows_b)
    send_e, send_o = pl.pallas_call(
        ghost_kernel,
        in_specs=[vmem] * 4,
        out_specs=[vmem] * 2,
        out_shape=[planes(3), planes(3)],
        name="pack_ghost_columns",
    )(columns_e, columns_o, recv_a, recv_b)
    recv_e = lax.ppermute(send_e, "ia", even)
    recv_o = lax.ppermute(send_o, "ia", odd)

    def fold_and_inner(q, send_b, raw):
        near = lax.ppermute(send_b, both, fold(q))
        far = lax.ppermute(send_b, both, fold((q - 1) % count))
        inner = pl.pallas_call(
            inner_kernel,
            in_specs=[hbm] * 4,
            out_specs=hbm,
            out_shape=planes(R - 6),
            scratch_shapes=[scratch(R - 6), pltpu.SemaphoreType.DMA] + RAW_SCRATCH,
            compiler_params=big,
            cost_estimate=cost(2 * 10**8, 16 * 10**6),
            name="inner",
        )(*raw)
        return near, far, inner

    near, far, inner = lax.switch(
        block, [functools.partial(fold_and_inner, q) for q in range(count)], send_b, raw
    )
    return pl.pallas_call(
        finish_kernel,
        in_specs=[hbm] * 5 + [vmem] + [hbm] * 8 + [vmem],
        out_specs=hbm,
        out_shape=jax.ShapeDtypeStruct((V, L, R, C), jnp.float32),
        scratch_shapes=[
            scratch(8), scratch(8), scratch(), scratch(3), scratch(3), scratch(8),
            scratch(3, PLANES), scratch(2, PLANES), scratch(R), scratch(R),
            pltpu.VMEM((V, SLOTS, C), jnp.float32), pltpu.VMEM((V, SLOTS, 2 * C), jnp.bfloat16),
            pltpu.SMEM((C,), jnp.int32), pltpu.SemaphoreType.DMA,
        ] + RAW_SCRATCH + [pltpu.SemaphoreType.DMA((7,)), pltpu.SemaphoreType.DMA((V,))],
        compiler_params=big,
        name="finish",
    )(
        *raw, inner, jnp.swapaxes(vertical, 0, 1), partner, strips,
        recv_a, recv_b, near, far, recv_e, recv_o, recv_x,
    )


def solution(mesh):
    placed = (
        P(None, None, "ja", "ia"),
        P(None, None, "ja", "ia"),
        P(None, None, "ja", "ia"),
        P(None, "ja", "ia"),
        P(),
        P(),
    )
    return jax.shard_map(
        body, mesh=mesh, in_specs=placed, out_specs=P(None, None, "ja", "ia"), check_vma=False
    )
```
